128 devices in a mesh: dp: 16 (over x, y), tensor: 8 (over z, core).
Axes of the slice: x: 4, y: 4, z: 4, core: 2. Of those that a mesh axis runs over, the one named last changes fastest.
Arguments:
- inputs: bfloat16 [16384, 2048], P('dp'), may hold values from -6 to 6
- doc_lengths: int32 [16, 4], P('dp'), may hold values from 1 to 512, 1024 in all within a row
- norm1_gain: float32 [2048], replicated, may hold values from 0.5 to 1.5
- w_query: bfloat16 [2048, 2048], P(None, 'tensor'), may hold values from -0.125 to 0.125
- w_shared_kv: bfloat16 [2048, 256], replicated, may hold values from -0.125 to 0.125
- w_output: bfloat16 [2048, 2048], P('tensor'), may hold values from -1.5 to 1.5
- norm2_gain: float32 [2048], replicated, may hold values from 0.5 to 1.5
- w_gate: bfloat16 [2048, 5632], P(None, 'tensor'), may hold values from -0.125 to 0.125
- w_up: bfloat16 [2048, 5632], P(None, 'tensor'), may hold values from -0.125 to 0.125
- w_down: bfloat16 [5632, 2048], P('tensor'), may hold values from -0.078125 to 0.078125
- out_cotangent: bfloat16 [16384, 2048], P('dp'), may hold values from -6 to 6
- kv_cotangent: float32 [16384, 256], P('dp'), may hold values from -6 to 6
Outputs:
- output: bfloat16 [16384, 2048], P('dp')
- input_grad: bfloat16 [16384, 2048], P('dp')
- shared_kv: bfloat16 [16384, 256], P('dp')
- grad_norm1: float32 [2048], P(('dp', 'tensor'))
- grad_query: float32 [2048, 2048], P('dp', 'tensor')
- grad_shared_kv: float32 [2048, 256], P(('dp', 'tensor'))
- grad_output: float32 [2048, 2048], P('tensor', 'dp')
- grad_norm2: float32 [2048], P(('dp', 'tensor'))
- grad_gate: float32 [2048, 5632], P('dp', 'tensor')
- grad_up: float32 [2048, 5632], P('dp', 'tensor')
- grad_down: float32 [5632, 2048], P('tensor', 'dp')
The draws below stay inside these ranges and needn't reach their ends.
Inputs may be any that keep to these rules, and one draw needn't show every extreme that they name: `doc_lengths`: each row holds the lengths of 4 documents packed in order into one sequence; a row sums to 1024, and its longest document has 512 tokens.
All inputs are finite; a program needn't handle non-finite values.
Results may differ from the reference program's by a relative error of at most 0.018.
Values may be sent and summed in bfloat16 or wider, within the bound.
A program may use at most 192 MiB of HBM per device.

```python
import math
import jax
import jax.numpy as jnp
import numpy as np
from jax import lax

D = 2048
H = 16
HD = 128
FF = 5632
SEQ_LEN = 1024
SEQS = 1
DOCS = 4
DOC_MOST = 512
TOKENS = 16384
N_DP = 16


def spiked(entries, rng, source, target, shards_of, factor):
    def block_of(dim):
        return (jnp.arange(entries.shape[dim]) // (entries.shape[dim] // shards_of)).reshape((-1,) + (1,) * (entries.ndim - 1 - dim))

    near = jax.random.permutation(rng, shards_of)[block_of(target)]
    other_side = (block_of(target) + shards_of // 2) % shards_of
    return jnp.where((block_of(source) == near) | (block_of(source) == other_side), factor * entries, entries)


def block_levels(rng, shape, pieces, smallest, high):
    loudness = 1.0
    for axis_at, blocks in pieces:
        steps = jax.random.uniform(jax.random.fold_in(jax.random.fold_in(rng, 6), axis_at), (blocks,), jnp.float32, smallest / len(pieces), high / len(pieces))
        loudness = loudness * jnp.repeat(jnp.exp(steps), shape[axis_at] // blocks).reshape((-1,) + (1,) * (len(shape) - 1 - axis_at))
    return loudness


def length_profile(count, total, reach, lean):
    portions = [(1 << 20) // math.isqrt(grade ** lean) + 1 for grade in range(2, count + 1)]
    surplus, given = total - reach - (count - 1), [1] * (count - 1)
    while surplus > 0:
        candidates = [i for i in range(count - 1) if given[i] < reach]
        pool, left = sum([portions[i] for i in candidates]), surplus
        for i in candidates:
            addition = min(reach - given[i], max(1, left * portions[i] // pool), surplus)
            given[i] = given[i] + addition
            surplus = surplus - addition
    return np.array([reach] + given)


def uneven_parts(key, amount, total, most, lean):
    if amount == 2:
        one = jax.random.randint(key, (), max(1, total - most), min(most, total - 1) + 1)
        return jnp.stack([one, total - one])
    lengths = jnp.asarray(length_profile(amount, total, most, lean), jnp.int32)
    couples = (amount - 1) // 2
    source_of, sink = lengths[1:1 + 2 * couples:2], lengths[2:2 + 2 * couples:2]
    slack = jnp.minimum(source_of - 1, most - sink)
    shifted = jax.random.randint(jax.random.fold_in(key, 1), (couples,), 0, 1 << 20) % (slack + 1)
    lengths = lengths.at[1:1 + 2 * couples:2].set(source_of - shifted).at[2:2 + 2 * couples:2].set(sink + shifted)
    return lengths[jax.random.permutation(jax.random.fold_in(key, 2), amount)]


def gaussian(key, shape, deviation, most, pieces=(), held_as=jnp.bfloat16):
    array = deviation * jax.random.normal(key, shape, jnp.float32)
    if pieces:
        array = array * block_levels(key, shape, pieces, -0.22, 0.18)
    return jnp.clip(array, -most, most).astype(held_as)


def heavy_noise(own_key, extent, deviation, reach, split, heavy, held_as=jnp.bfloat16):
    values = deviation * jax.random.normal(own_key, extent, jnp.float32)
    if split:
        values = values * block_levels(own_key, extent, split, -0.22, 0.18)
    return jnp.clip(spiked(values, jax.random.fold_in(own_key, 3), *heavy), -reach, reach).astype(held_as)


def setup_inputs(seed: int = 0) -> dict:
    seeds = jax.random.split(jax.random.key(seed), 13)
    inputs = heavy_noise(seeds[0], (TOKENS, D), 1.0, 6.0, ((0, 16),), (0, 1, 16, 2.0))
    doc_lengths = jax.vmap(lambda own: uneven_parts(own, DOCS, SEQ_LEN, DOC_MOST, 2))(jax.random.split(seeds[1], (SEQS * N_DP))).reshape((SEQS * N_DP, DOCS)).astype(jnp.int32)
    norm1_gain = jnp.clip(1.0 + 0.1 * jax.random.normal(seeds[2], (D,), jnp.float32), 0.5, 1.5)
    w_query = gaussian(seeds[3], (D, H * HD), D ** -0.5, 0.125, ((1, 8),))
    w_shared_kv = gaussian(seeds[4], (D, 2 * HD), D ** -0.5, 0.125)
    w_output = gaussian(seeds[5], (H * HD, D), (4 * H * HD // DOC_MOST) ** -0.5, 1.5, ((0, 8),))
    norm2_gain = jnp.clip(1.0 + 0.1 * jax.random.normal(seeds[6], (D,), jnp.float32), 0.5, 1.5)
    w_gate = gaussian(seeds[7], (D, FF), D ** -0.5, 0.125, ((1, 8),))
    w_up = gaussian(seeds[8], (D, FF), D ** -0.5, 0.125, ((1, 8),))
    w_down = gaussian(seeds[9], (FF, D), FF ** -0.5, 0.078125, ((0, 8),))
    out_cotangent = heavy_noise(seeds[10], (TOKENS, D), 1.0, 6.0, ((0, 16),), (0, 1, 16, 2.0))
    kv_cotangent = gaussian(seeds[11], (TOKENS, 2 * HD), 1.0, 6.0, ((0, 16),), jnp.float32)
    return dict(inputs=inputs, doc_lengths=doc_lengths, norm1_gain=norm1_gain, w_query=w_query, w_shared_kv=w_shared_kv, w_output=w_output, norm2_gain=norm2_gain, w_gate=w_gate, w_up=w_up, w_down=w_down, out_cotangent=out_cotangent, kv_cotangent=kv_cotangent)


EPSILON = 1e-05
NEGATIVE = -1e+30
HIGHEST = lax.Precision.HIGHEST

@jax.custom_vjp
def low(v):
    return lax.optimization_barrier(v.astype(jnp.bfloat16)).astype(jnp.float32)

@jax.custom_vjp
def low_back(v):
    return v

def low_keep(v):
    return (low(v), None)

def low_pass(kept, grad):
    return (grad,)

def back_keep(v):
    return (v, None)

def back_low(kept, grad):
    return (low(grad),)
low.defvjp(low_keep, low_pass)
low_back.defvjp(back_keep, back_low)

def positions_of(doc_lengths, seq_len):
    ends = jnp.cumsum(doc_lengths, axis=1, dtype=jnp.int32)
    starts = ends - doc_lengths
    offsets = jnp.arange(seq_len, dtype=jnp.int32)
    segment = lax.optimization_barrier(jnp.sum((offsets[None, :, None] >= ends[:, None, :]).astype(jnp.int32), axis=2, dtype=jnp.int32))
    labels = jnp.arange(doc_lengths.shape[1], dtype=jnp.int32)
    chosen = segment[:, :, None] == labels[None, None, :]
    first_row = lax.optimization_barrier(jnp.sum(jnp.where(chosen, starts[:, None, :], 0), axis=2, dtype=jnp.int32))
    return (segment, offsets[None, :] - first_row)

def rope_tables(position, head_dim):
    counter = jnp.arange(head_dim // 2, dtype=jnp.float32)
    inverse = jnp.exp(counter * (-2.0 * math.log(10000.0) / head_dim))
    angle = position.astype(jnp.float32)[..., None] * inverse
    return (jnp.cos(angle), jnp.sin(angle))

def rotate(values, cosine, sine):
    middle = values.shape[-1] // 2
    former = values[..., :middle]
    latter = values[..., middle:]
    return jnp.concatenate([former * cosine - latter * sine, latter * cosine + former * sine], axis=-1)

def normalize(values):
    factor = lax.rsqrt(lax.optimization_barrier(jnp.mean(values * values, axis=-1, keepdims=True)) + EPSILON)
    return (values * factor, factor)

def allowed_of(segment_row):
    offsets = jnp.arange(segment_row.shape[0], dtype=jnp.int32)
    same_doc = segment_row[:, None] == segment_row[None, :]
    return same_doc & (offsets[:, None] >= offsets[None, :])

def forward(params, inputs_seq, segment_row, position_row):
    norm1_g, query_w, kv_w, output_w, norm2_g, gate_w, up_w, down_w = params
    head_dim = kv_w.shape[1] // 2
    heads = query_w.shape[1] // head_dim
    length = inputs_seq.shape[0]
    cosine, sine = rope_tables(position_row, head_dim)
    normed1, factor1 = normalize(inputs_seq)
    n1_low = low(normed1 * norm1_g)
    query = low_back(jnp.dot(n1_low, query_w, precision=HIGHEST))
    kv_pre = low_back(jnp.dot(n1_low, kv_w, precision=HIGHEST))
    query_rot = low(rotate(query.reshape(length, heads, head_dim), cosine[:, None, :], sine[:, None, :]))
    key_rot = low(rotate(kv_pre[:, :head_dim], cosine, sine))
    value_low = low(kv_pre[:, head_dim:])
    factor = 1.0 / math.sqrt(head_dim)
    scores = low_back(jnp.einsum('qhd,kd->hqk', query_rot, key_rot, precision=HIGHEST) * factor)
    scores = jnp.where(allowed_of(segment_row)[None], scores, NEGATIVE)
    highest = lax.optimization_barrier(jnp.max(scores, axis=-1, keepdims=True))
    log_total = highest + jnp.log(lax.optimization_barrier(jnp.sum(jnp.exp(scores - highest), axis=-1, keepdims=True)))
    weights = low(jnp.exp(scores - log_total))
    attended = jnp.einsum('hqk,kd->qhd', weights, value_low, precision=HIGHEST)
    attended = low(low_back(attended)).reshape(length, heads * head_dim)
    hidden1 = inputs_seq + low_back(jnp.dot(attended, output_w, precision=HIGHEST))
    normed2, factor2 = normalize(hidden1)
    n2_low = low(normed2 * norm2_g)
    gate_pre = low_back(jnp.dot(n2_low, gate_w, precision=HIGHEST))
    up_pre = low_back(jnp.dot(n2_low, up_w, precision=HIGHEST))
    hidden = low(gate_pre * jax.nn.sigmoid(gate_pre) * up_pre)
    output = hidden1 + low_back(jnp.dot(hidden, down_w, precision=HIGHEST))
    return (output, jnp.concatenate([key_rot, value_low], axis=-1))

def add_pair(former, latter):
    return former + latter

def reference(inputs, doc_lengths, norm1_gain, w_query, w_shared_kv, w_output, norm2_gain, w_gate, w_up, w_down, out_cotangent, kv_cotangent):
    params = tuple((value.astype(jnp.float32) for value in (norm1_gain, w_query, w_shared_kv, w_output, norm2_gain, w_gate, w_up, w_down)))
    width = inputs.shape[1]
    seq_total = doc_lengths.shape[0]
    seq_len = inputs.shape[0] // seq_total
    stacked_in = inputs.astype(jnp.float32).reshape(seq_total, seq_len, width)
    stacked_out = out_cotangent.astype(jnp.float32).reshape(seq_total, seq_len, width)
    stacked_kv = kv_cotangent.astype(jnp.float32).reshape(seq_total, seq_len, kv_cotangent.shape[1])

    def one_sequence(totals, operands):
        inputs_seq, lengths_row, out_ct, kv_ct = operands
        segment, position = positions_of(lengths_row[None, :], seq_len)

        def layer(param_set, values):
            return forward(param_set, values, segment[0], position[0])
        (output_seq, shared_seq), pull = jax.vjp(layer, params, inputs_seq)
        grad_params, grad_inputs = pull((out_ct, kv_ct))
        totals = jax.tree.map(add_pair, totals, grad_params)
        return (totals, (output_seq.astype(jnp.bfloat16), grad_inputs.astype(jnp.bfloat16), shared_seq.astype(jnp.bfloat16)))
    initial = jax.tree.map(jnp.zeros_like, params)
    grads, (outputs, input_grads, shared) = lax.scan(one_sequence, initial, (stacked_in, doc_lengths, stacked_out, stacked_kv))
    tokens_all = seq_total * seq_len
    return (outputs.reshape(tokens_all, width), input_grads.reshape(tokens_all, width), shared.reshape(tokens_all, shared.shape[2]), grads[0], grads[1], grads[2], grads[3], grads[4], grads[5], grads[6], grads[7])
```

```python
import functools
import math

import jax
import jax.numpy as jnp
from jax import lax
from jax.experimental import pallas as pl
from jax.experimental.pallas import tpu as pltpu
from jax.sharding import PartitionSpec as P

EPSILON = 1e-05
NEGATIVE = -1e30
MESH = pl.DeviceIdType.MESH
F32, BF16 = jnp.float32, jnp.bfloat16
VM = pl.BlockSpec(memory_space=pltpu.VMEM)
ANY = pl.BlockSpec(memory_space=pl.ANY)


class Links:
    def __init__(self, send, recv):
        dp, t = lax.axis_index("dp"), lax.axis_index("tensor")
        self.dp, self.t = dp, t
        self.x, self.y, self.z, self.c = dp // 4, dp % 4, t // 2, t % 2
        self.send, self.recv, self.used = send, recv, 0
        self.sent = []

    def slot(self, d, c=None):
        return 2 * ((self.z + d) % 4) + (self.c if c is None else c)

    def zdev(self, d):
        return (self.dp, self.slot(d))

    def sib(self):
        return (self.dp, self.slot(0, 1 - self.c))

    def xdev(self, d):
        return (((self.x + d) % 4) * 4 + self.y, self.t)

    def ydev(self, d):
        return (self.x * 4 + (self.y + d) % 4, self.t)

    def barrier(self, devs):
        b = pltpu.get_barrier_semaphore()
        for dev in devs:
            pl.semaphore_signal(b, inc=1, device_id=dev, device_id_type=MESH)
        pl.semaphore_wait(b, len(devs))

    def cp(self, src, dst, dev):
        copy = pltpu.make_async_remote_copy(
            src_ref=src,
            dst_ref=dst,
            send_sem=self.send.at[self.used],
            recv_sem=self.recv.at[self.used],
            device_id=dev,
            device_id_type=MESH,
        )
        self.used += 1
        copy.start()
        self.sent.append(copy)
        return copy

    def drain(self):
        for copy in self.sent:
            copy.wait_send()
        self.sent = []


def slabs(rows, step, body):
    if rows == step:
        body(pl.ds(0, step))
        return

    def one(i, carry):
        body(pl.ds(pl.multiple_of(i * step, step), step))
        return carry

    lax.fori_loop(0, rows // step, one, 0)


def add_rows(dst, src, rows, step=32):
    def body(s):
        dst[s] = dst[s] + src[s]

    slabs(rows, step, body)


def rs_z(k, part, rc, acc, hp, hm, fp, fm):
    order = (2, 1, 3, 0)
    swap = [k.cp(part.at[k.slot(d, 1 - k.c)], rc.at[i], k.sib()) for i, d in enumerate(order)]

    def core_add(i):
        swap[i].wait_recv()
        mine = part.at[k.slot(order[i])]

        def body(s):
            acc[i, s] = mine[s] + rc[i, s]

        slabs(128, 32, body)

    lo, hi = pl.ds(0, 64), pl.ds(64, 64)
    core_add(0)
    h1 = k.cp(acc.at[0, lo], hp, k.zdev(1))
    h2 = k.cp(acc.at[0, hi], hm, k.zdev(-1))
    core_add(1)
    u1 = k.cp(acc.at[1, hi], fp.at[hi], k.zdev(1))
    core_add(2)
    u2 = k.cp(acc.at[2, lo], fm.at[lo], k.zdev(-1))
    h1.wait_recv()
    add_rows(acc.at[1, lo], hp, 64)
    w1 = k.cp(acc.at[1, lo], fp.at[lo], k.zdev(1))
    h2.wait_recv()
    add_rows(acc.at[2, hi], hm, 64)
    w2 = k.cp(acc.at[2, hi], fm.at[hi], k.zdev(-1))
    core_add(3)
    for copy in (u1, u2, w1, w2):
        copy.wait_recv()


def ag_z(k, dst):
    lo, hi = pl.ds(0, 64), pl.ds(64, 64)
    me, below, above, far = k.t, k.slot(-1), k.slot(1), k.slot(2)
    a1 = k.cp(dst.at[me, lo], dst.at[me, lo], k.zdev(1))
    b1 = k.cp(dst.at[me, hi], dst.at[me, hi], k.zdev(-1))
    a2 = k.cp(dst.at[me, hi], dst.at[me, hi], k.zdev(1))
    b2 = k.cp(dst.at[me, lo], dst.at[me, lo], k.zdev(-1))
    s0 = k.cp(dst.at[me], dst.at[me], k.sib())
    a1.wait_recv()
    f1 = k.cp(dst.at[below, lo], dst.at[below, lo], k.zdev(1))
    b1.wait_recv()
    f2 = k.cp(dst.at[above, hi], dst.at[above, hi], k.zdev(-1))
    a2.wait_recv()
    s1 = k.cp(dst.at[below], dst.at[below], k.sib())
    b2.wait_recv()
    s2 = k.cp(dst.at[above], dst.at[above], k.sib())
    f1.wait_recv()
    f2.wait_recv()
    s3 = k.cp(dst.at[far], dst.at[far], k.sib())
    for copy in (s0, s1, s2, s3):
        copy.wait_recv()


def z_scratch(width):
    return [
        pltpu.VMEM((4, 128, width), BF16),
        pltpu.VMEM((4, 128, width), BF16),
        pltpu.VMEM((64, width), BF16),
        pltpu.VMEM((64, width), BF16),
        pltpu.VMEM((128, width), BF16),
        pltpu.VMEM((128, width), BF16),
    ]


def sems(n):
    return [pltpu.SemaphoreType.DMA((n,)), pltpu.SemaphoreType.DMA((n,))]


def own_sum(acc, fp, fm, s):
    return acc[3, s].astype(F32) + fp[s].astype(F32) + fm[s].astype(F32)


def z_barrier(k):
    k.barrier([k.zdev(1), k.zdev(-1), k.sib()])


def unit(values):
    factor = lax.rsqrt(jnp.mean(values * values, axis=-1, keepdims=True) + EPSILON)
    return values * factor, factor


def h1_kernel(part, x, gain, h1_out, n2_out, rc, acc, hp, hm, fp, fm, send, recv):
    k = Links(send, recv)
    z_barrier(k)
    rs_z(k, part, rc, acc, hp, hm, fp, fm)

    def body(s):
        h1 = x[k.t, s].astype(F32) + own_sum(acc, fp, fm, s)
        h1_out[s] = h1
        n2_out[k.t, s] = (unit(h1)[0] * gain[...]).astype(BF16)

    slabs(128, 16, body)
    ag_z(k, n2_out)
    k.drain()


def out_kernel(part, h1, y_out, rc, acc, hp, hm, fp, fm, send, recv):
    k = Links(send, recv)
    z_barrier(k)
    rs_z(k, part, rc, acc, hp, hm, fp, fm)

    def body(s):
        y_out[k.t, s] = (h1[s] + own_sum(acc, fp, fm, s)).astype(BF16)

    slabs(128, 16, body)
    ag_z(k, y_out)
    k.drain()


def norm_back(d_normed, gain, normed, factor):
    scaled = d_normed * gain
    return factor * (scaled - normed * jnp.mean(scaled * normed, axis=-1, keepdims=True))


def dn2_kernel(part, oc, h1, gain, dh1_out, db_out, gnorm, rc, acc, hp, hm, fp, fm, send, recv):
    k = Links(send, recv)
    z_barrier(k)
    rs_z(k, part, rc, acc, hp, hm, fp, fm)
    gnorm[...] = jnp.zeros_like(gnorm)

    def body(s):
        d = own_sum(acc, fp, fm, s)
        y2, r2 = unit(h1[s])
        dh1 = oc[k.t, s].astype(F32) + norm_back(d, gain[...], y2, r2)
        dh1_out[s] = dh1
        db_out[k.t, s] = dh1.astype(BF16)
        dy = d * y2
        gnorm[...] += dy[0:8] + dy[8:16]

    slabs(128, 16, body)
    ag_z(k, db_out)
    k.drain()


def dot(a, b, dims=((1,), (0,))):
    return lax.dot_general(a, b, (dims, ((), ())), preferred_element_type=F32)


def rope_cols(values, cos, sin):
    return values * cos + pltpu.roll(values, 64, axis=1) * sin


def dn1_kernel(
    part, kvpart, kvct, cos, sin, wkv, x, dh1, gain, n1,
    ig_out, gkv_out, gnorm,
    rc, acc, hp, hm, fp, fm, kvrc, kvacc, kvin, dkv, send, recv,
):
    k = Links(send, recv)
    k.barrier([k.zdev(1), k.zdev(-1), k.zdev(2), k.sib()])
    swap = k.cp(kvpart.at[1 - k.c], kvrc, k.sib())
    rs_z(k, part, rc, acc, hp, hm, fp, fm)
    swap.wait_recv()
    kvacc[...] = kvpart[k.c] + kvrc[...]
    got = [
        k.cp(kvacc.at[(k.z + d) % 4], kvin.at[d - 1], k.zdev(d)) for d in (1, 2, 3)
    ]
    for copy in got:
        copy.wait_recv()
    total = kvacc[k.z].astype(F32) + kvct[k.t]
    for d in range(3):
        total = total + kvin[d].astype(F32)
    dkv[:, 0:128] = rope_cols(total[:, 0:128], cos[k.t], -sin[k.t]).astype(BF16)
    dkv[:, 128:256] = total[:, 128:256].astype(BF16)
    gkv_out[...] = dot(n1[k.t], dkv[...], ((0,), (0,))).astype(BF16)
    gnorm[...] = jnp.zeros_like(gnorm)

    def body(s):
        d = own_sum(acc, fp, fm, s) + dot(dkv[s], wkv[...], ((1,), (1,)))
        y1, r1 = unit(x[k.t, s].astype(F32))
        ig_out[k.t, s] = (dh1[s] + norm_back(d, gain[...], y1, r1)).astype(BF16)
        dy = d * y1
        gnorm[...] += dy[0:8] + dy[8:16]

    slabs(128, 16, body)
    ag_z(k, ig_out)
    k.drain()


def rs4(k, view, hp, hm, fp, fm, dev, halves, add, fin):
    h1 = k.cp(view(2, 0), hp, dev(1))
    h2 = k.cp(view(2, 1), hm, dev(-1))
    u1 = k.cp(view(1, 1), halves(fp, 1), dev(1))
    u2 = k.cp(view(3, 0), halves(fm, 0), dev(-1))
    yield
    h1.wait_recv()
    add(view(1, 0), hp)
    w1 = k.cp(view(1, 0), halves(fp, 0), dev(1))
    h2.wait_recv()
    add(view(3, 1), hm)
    w2 = k.cp(view(3, 1), halves(fm, 1), dev(-1))
    yield
    for copy in (u1, w1, u2, w2):
        copy.wait_recv()
    fin()


def add3(dst, a, b):
    dst[...] = (dst[...].astype(F32) + a[...].astype(F32) + b[...].astype(F32)).astype(dst.dtype)


def gr_kernel(
    g_in, kv_in, g_out, kv_out,
    g, hp1, hm1, fp1, fm1, hp2, hm2, fp2, fm2, kvrc, kvacc, kvz, kvx, kvy, copy_sem, send, recv,
):
    R = g.shape[2]
    H, Q = R // 2, R // 4
    k = Links(send, recv)
    load = pltpu.make_async_copy(g_in, g, copy_sem)
    load.start()
    k.barrier(
        [k.sib()] + [dev(d) for dev in (k.xdev, k.ydev, k.zdev) for d in (1, 2, 3)]
    )
    swap = k.cp(kv_in.at[:, pl.ds(4 * (1 - k.c), 4)], kvrc, k.sib())
    load.wait()

    def wide_half(f, h):
        return f.at[pl.ds(2 * h, 2)]

    def wide_add(dst, src):
        for i in range(2):
            slabs(H, Q, lambda s: dst.__setitem__((i, s), dst[i, s] + src[i, s]))

    def thin_half(f, h):
        return f.at[0, pl.ds(Q * h, Q)]

    def thin_add(dst, src):
        slabs(Q, Q, lambda s: dst.__setitem__(s, dst[s] + src[s]))

    def wide_fin(own, fp, fm):
        def fin():
            for i in range(4):
                def body(s):
                    own(i)[s] = (own(i)[s].astype(F32) + fp[i, s].astype(F32) + fm[i, s].astype(F32)).astype(BF16)
                slabs(H, Q, body)
        return fin

    def thin_fin(own, fp, fm, at):
        def fin():
            def body(s):
                g_out[pl.ds(at + s.start, s.size)] = (
                    own[s].astype(F32) + fp[0, s].astype(F32) + fm[0, s].astype(F32)
                )
            slabs(H, Q, body)
        return fin

    first = pl.ds(0, H)
    second = pl.ds(H, H)
    a1 = rs4(
        k, lambda d, h: g.at[(k.x + d) % 4, pl.ds(2 * h, 2), first],
        hp1, hm1, fp1, fm1, k.xdev, wide_half, wide_add,
        wide_fin(lambda i: g.at[k.x, i, first], fp1, fm1),
    )
    b1 = rs4(
        k, lambda d, h: g.at[pl.ds(2 * h, 2), (k.y + d) % 4, second],
        hp2, hm2, fp2, fm2, k.ydev, wide_half, wide_add,
        wide_fin(lambda i: g.at[i, k.y, second], fp2, fm2),
    )
    next(a1); next(b1)
    swap.wait_recv()
    for i in range(16):
        kvacc[i] = kv_in[i, pl.ds(4 * k.c, 4)] + kvrc[i]
    next(a1); next(b1)
    zin = [k.cp(kvacc.at[:, (k.z + d) % 4], kvz.at[d - 1], k.zdev(d)) for d in (1, 2, 3)]
    for copy in zin:
        copy.wait_recv()
    kvz[3] = kvacc[:, k.z]
    kvz[3] = (sum(kvz[i].astype(F32) for i in range(4))).astype(BF16)
    for p in (a1, b1):
        for _ in p:
            pass
    xin = [k.cp(kvz.at[3, pl.ds(4 * ((k.x + d) % 4), 4)], kvx.at[d - 1], k.xdev(d)) for d in (1, 2, 3)]
    return k, xin


def body_gr(*refs):
    (g_in, kv_in, g_out, kv_out, g, hp1, hm1, fp1, fm1, hp2, hm2, fp2, fm2,
     kvrc, kvacc, kvz, kvx, kvy, tp1, tm1, tq1, tr1, tp2, tm2, tq2, tr2, copy_sem, send, recv) = refs
    k, xin = gr_kernel(
        g_in, kv_in, g_out, kv_out, g, hp1, hm1, fp1, fm1, hp2, hm2, fp2, fm2,
        kvrc, kvacc, kvz, kvx, kvy, copy_sem, send, recv)
    R = g.shape[2]
    H, Q = R // 2, R // 4

    def thin_half(f, h):
        return f.at[pl.ds(Q * h, Q)]

    def thin_add(dst, src):
        slabs(Q, Q, lambda s: dst.__setitem__(s, dst[s] + src[s]))

    def thin_fin(own, fp, fm, at):
        def fin():
            def body(i, carry):
                s = pl.ds(pl.multiple_of(i * Q, Q), Q)
                o = pl.ds(pl.multiple_of(at + i * Q, 8), Q)
                g_out[o] = own[s].astype(F32) + fp[s].astype(F32) + fm[s].astype(F32)
                return carry
            lax.fori_loop(0, 2, body, 0)
        return fin

    a2 = rs4(
        k, lambda d, h: g.at[k.x, (k.y + d) % 4, pl.ds(Q * h, Q)],
        tp1, tm1, tq1, tr1, k.ydev, thin_half, thin_add,
        thin_fin(g.at[k.x, k.y, pl.ds(0, H)], tq1, tr1, 0),
    )
    b2 = rs4(
        k, lambda d, h: g.at[(k.x + d) % 4, k.y, pl.ds(H + Q * h, Q)],
        tp2, tm2, tq2, tr2, k.xdev, thin_half, thin_add,
        thin_fin(g.at[k.x, k.y, pl.ds(H, H)], tq2, tr2, H),
    )
    next(a2); next(b2)
    for copy in xin:
        copy.wait_recv()
    kvx[3] = (kvz[3, pl.ds(4 * k.x, 4)].astype(F32) + sum(kvx[i].astype(F32) for i in range(3))).astype(BF16)
    yin = [k.cp(kvx.at[3, (k.y + d) % 4], kvy.at[d - 1], k.ydev(d)) for d in (1, 2, 3)]
    next(a2); next(b2)
    for copy in yin:
        copy.wait_recv()
    kv_out[...] = kvx[3, k.y].astype(F32) + sum(kvy[i].astype(F32) for i in range(3))
    for p in (a2, b2):
        for _ in p:
            pass
    k.drain()


def call(kernel, cid, outs, ins, scratch, in_specs=None, limit=60):
    return pl.pallas_call(
        kernel,
        out_shape=[jax.ShapeDtypeStruct(s, d) for s, d in outs],
        in_specs=in_specs or [VM] * len(ins),
        out_specs=[VM] * len(outs),
        scratch_shapes=scratch,
        compiler_params=pltpu.CompilerParams(
            collective_id=cid, has_side_effects=True, vmem_limit_bytes=limit * 2**20
        ),
    )(*ins)


def positions_of(doc_lengths, seq_len):
    ends = jnp.cumsum(doc_lengths, axis=1, dtype=jnp.int32)
    starts = ends - doc_lengths
    offsets = jnp.arange(seq_len, dtype=jnp.int32)
    segment = jnp.sum(
        (offsets[None, :, None] >= ends[:, None, :]).astype(jnp.int32), axis=2, dtype=jnp.int32
    )
    labels = jnp.arange(doc_lengths.shape[1], dtype=jnp.int32)
    chosen = segment[:, :, None] == labels[None, None, :]
    first_row = jnp.sum(jnp.where(chosen, starts[:, None, :], 0), axis=2, dtype=jnp.int32)
    return (segment, offsets[None, :] - first_row)


def rope_tables(position, head_dim):
    counter = jnp.arange(head_dim // 2, dtype=jnp.float32)
    inverse = jnp.exp(counter * (-2.0 * math.log(10000.0) / head_dim))
    angle = position.astype(jnp.float32)[..., None] * inverse
    return (jnp.cos(angle), jnp.sin(angle))


def rotate(values, cosine, sine):
    middle = values.shape[-1] // 2
    former = values[..., :middle]
    latter = values[..., middle:]
    return jnp.concatenate(
        [former * cosine - latter * sine, latter * cosine + former * sine], axis=-1
    )


def masked_scores(query_seq, key_seq, segment_row):
    offsets = jnp.arange(segment_row.shape[0], dtype=jnp.int32)
    allowed = (segment_row[:, None] == segment_row[None, :]) & (offsets[:, None] >= offsets[None, :])
    factor = 1.0 / math.sqrt(query_seq.shape[-1])
    scores = jnp.einsum("qhd,kd->hqk", query_seq, key_seq, preferred_element_type=F32) * factor
    return jnp.where(allowed[None], scores, NEGATIVE)


def per_device(
    inputs, doc_lengths, norm1_gain, w_query, w_shared_kv, w_output, norm2_gain,
    w_gate, w_up, w_down, out_cotangent, kv_cotangent,
):
    segment, position = positions_of(doc_lengths, 1024)
    segment = segment[0]
    cosine, sine = rope_tables(position[0], 128)
    head_cos, head_sin = cosine[:, None, :], sine[:, None, :]
    x = inputs.astype(F32)
    y1, r1 = unit(x)
    n1 = (y1 * norm1_gain).astype(BF16)
    query = jnp.dot(n1, w_query, preferred_element_type=F32)
    kv_pre = jnp.dot(n1, w_shared_kv, preferred_element_type=F32)
    query_rot = rotate(query.reshape(1024, 2, 128), head_cos, head_sin).astype(BF16)
    key_rot = rotate(kv_pre[:, :128], cosine, sine).astype(BF16)
    value = kv_pre[:, 128:].astype(BF16)
    shared_kv = jnp.concatenate([key_rot, value], axis=-1)
    scores = masked_scores(query_rot, key_rot, segment)
    highest = jnp.max(scores, axis=-1, keepdims=True)
    grown = jnp.exp(scores - highest)
    probs = grown / jnp.sum(grown, axis=-1, keepdims=True)
    probs_low = probs.astype(BF16)
    attended = jnp.einsum("hqk,kd->qhd", probs_low, value, preferred_element_type=F32)
    attended = attended.astype(BF16).reshape(1024, 256)
    part = jnp.dot(attended, w_output, preferred_element_type=F32).astype(BF16)
    gain1, gain2 = norm1_gain.reshape(1, 2048), norm2_gain.reshape(1, 2048)
    cut = lambda v: v.reshape(8, 128, v.shape[-1])
    wide = ((8, 128, 2048), BF16)
    shard = ((128, 2048), F32)
    h1, n2 = call(h1_kernel, 0, [shard, wide], [cut(part), cut(inputs), gain2], z_scratch(2048) + sems(24))
    n2 = n2.reshape(1024, 2048)
    gate = jnp.dot(n2, w_gate, preferred_element_type=F32)
    up = jnp.dot(n2, w_up, preferred_element_type=F32)
    sig = jax.nn.sigmoid(gate)
    silu = gate * sig
    hidden = (silu * up).astype(BF16)
    part = jnp.dot(hidden, w_down, preferred_element_type=F32).astype(BF16)
    (output,) = call(out_kernel, 1, [wide], [cut(part), h1], z_scratch(2048) + sems(24))
    d_hidden = jnp.dot(out_cotangent, w_down.T, preferred_element_type=F32)
    g_down = jnp.dot(hidden.T, out_cotangent, preferred_element_type=F32).astype(BF16)
    d_gate = (d_hidden * up * sig * (1.0 + gate * (1.0 - sig))).astype(BF16)
    d_up = (d_hidden * silu).astype(BF16)
    g_gate = jnp.dot(d_gate.T, n2, preferred_element_type=F32).astype(BF16)
    g_up = jnp.dot(d_up.T, n2, preferred_element_type=F32).astype(BF16)
    part = (
        jnp.dot(d_gate, w_gate.T, preferred_element_type=F32)
        + jnp.dot(d_up, w_up.T, preferred_element_type=F32)
    ).astype(BF16)
    dh1, db, gn2 = call(
        dn2_kernel, 2, [shard, wide, ((8, 2048), F32)],
        [cut(part), cut(out_cotangent), h1, gain2], z_scratch(2048) + sems(24),
    )
    db = db.reshape(1024, 2048)
    g_out = jnp.dot(attended.T, db, preferred_element_type=F32).astype(BF16)
    d_att = jnp.dot(db, w_output.T, preferred_element_type=F32).astype(BF16).reshape(1024, 2, 128)
    d_probs = jnp.einsum("qhd,kd->hqk", d_att, value, preferred_element_type=F32)
    delta = jnp.sum(probs * d_probs, axis=-1, keepdims=True)
    d_scores = (probs * (d_probs - delta)).astype(BF16)
    factor = 1.0 / math.sqrt(128)
    d_query = jnp.einsum("hqk,kd->qhd", d_scores, key_rot, preferred_element_type=F32) * factor
    d_key = jnp.einsum("hqk,qhd->kd", d_scores, query_rot, preferred_element_type=F32) * factor
    d_value = jnp.einsum("hqk,qhd->kd", probs_low, d_att, preferred_element_type=F32)
    kvpart = jnp.concatenate([d_key, d_value], axis=-1).astype(BF16)
    kvpart = kvpart.reshape(4, 2, 128, 256).transpose(1, 0, 2, 3)
    d_query = rotate(d_query, head_cos, -head_sin).astype(BF16).reshape(1024, 256)
    g_query = jnp.dot(d_query.T, n1, preferred_element_type=F32).astype(BF16)
    part = jnp.dot(d_query, w_query.T, preferred_element_type=F32).astype(BF16)
    cos2 = jnp.concatenate([cosine, cosine], axis=-1)
    sin2 = jnp.concatenate([-sine, sine], axis=-1)
    kv4 = pltpu.VMEM((4, 128, 256), BF16)
    input_grad, gkv, gn1 = call(
        dn1_kernel, 3, [wide, ((2048, 256), BF16), ((8, 2048), F32)],
        [cut(part), kvpart, cut(kv_cotangent), cut(cos2), cut(sin2), w_shared_kv, cut(inputs), dh1, gain1, cut(n1)],
        z_scratch(2048) + [kv4, kv4, pltpu.VMEM((3, 128, 256), BF16), pltpu.VMEM((128, 256), BF16)] + sems(32),
    )
    gn = [jnp.broadcast_to(jnp.sum(v, axis=0)[:, None], (2048, 64)).astype(BF16) for v in (gn1, gn2)]
    kvall = jnp.concatenate([gkv] + gn, axis=-1).reshape(16, 8, 16, 384)
    kvall = kvall.reshape(16, 4, 2, 16, 384).transpose(0, 2, 1, 3, 4).reshape(16, 8, 16, 384)
    pieces = lambda v: v.reshape(v.shape[0], 16, 128).transpose(1, 0, 2)
    g = jnp.concatenate([pieces(v) for v in (g_down, g_gate, g_up, g_out, g_query)], axis=1)
    R = 2624
    H, Q = R // 2, R // 4
    b = lambda *s: pltpu.VMEM(s, BF16)
    gsum, kvsum = call(
        body_gr, 4, [((R, 128), F32), ((16, 384), F32)], [g.reshape(4, 4, R, 128), kvall],
        [b(4, 4, R, 128)]
        + [b(2, H, 128), b(2, H, 128), b(4, H, 128), b(4, H, 128)] * 2
        + [b(16, 4, 16, 384), b(16, 4, 16, 384), b(4, 16, 16, 384), b(4, 4, 16, 384), b(3, 16, 384)]
        + [b(Q, 128), b(Q, 128), b(H, 128), b(H, 128)] * 2
        + [pltpu.SemaphoreType.DMA] + sems(48),
        in_specs=[ANY, VM],
    )
    return (
        output.reshape(1024, 2048),
        input_grad.reshape(1024, 2048),
        shared_kv,
        kvsum[:, 256],
        gsum[2368:2624].T,
        kvsum[:, 0:256],
        gsum[2112:2368],
        kvsum[:, 320],
        gsum[704:1408].T,
        gsum[1408:2112].T,
        gsum[0:704],
    )


def solution(mesh):
    placed = (
        P("dp", None), P("dp", None), P(), P(None, "tensor"), P(), P("tensor", None), P(),
        P(None, "tensor"), P(None, "tensor"), P("tensor", None), P("dp", None), P("dp", None),
    )
    return jax.shard_map(
        per_device,
        mesh=mesh,
        in_specs=placed,
        out_specs=(
            P("dp", None), P("dp", None), P("dp", None), P(("dp", "tensor")), P("dp", "tensor"),
            P(("dp", "tensor"), None), P("tensor", "dp"), P(("dp", "tensor")), P("dp", "tensor"),
            P("dp", "tensor"), P("tensor", "dp"),
        ),
        check_vma=False,
    )
```

```python
import math

import jax
import jax.numpy as jnp
import numpy as np
from jax import lax
from jax.experimental import pallas as pl
from jax.experimental.pallas import tpu as pltpu
from jax.sharding import PartitionSpec as P

EPSILON = 1e-05
NEGATIVE = -1e30
SCALE = 1.0 / math.sqrt(128)
MESH = pl.DeviceIdType.MESH
F32, BF16 = jnp.float32, jnp.bfloat16
VM = pl.BlockSpec(memory_space=pltpu.VMEM)
ANY = pl.BlockSpec(memory_space=pl.ANY)
NN, NT, TN = ((1,), (0,)), ((1,), (1,)), ((0,), (0,))
LO, HI = pl.ds(0, 64), pl.ds(64, 64)


def dot(a, b, dims=NN):
    return lax.dot_general(a, b, (dims, ((), ())), preferred_element_type=F32)


def loop(count, body):
    def one(i, carry):
        body(i)
        return carry

    lax.fori_loop(0, count, one, 0)


def rows(i, step):
    return pl.ds(pl.multiple_of(i * step, step), step)


class Links:
    def __init__(self, send, recv):
        dp, t = lax.axis_index("dp"), lax.axis_index("tensor")
        self.dp, self.t = dp, t
        self.x, self.y, self.z, self.c = dp // 4, dp % 4, t // 2, t % 2
        self.send, self.recv, self.used = send, recv, 0

    def slot(self, d, c=None):
        return 2 * ((self.z + d) % 4) + (self.c if c is None else c)

    def zdev(self, d):
        return (self.dp, self.slot(d))

    def sib(self):
        return (self.dp, self.slot(0, 1 - self.c))

    def xdev(self, d):
        return (((self.x + d) % 4) * 4 + self.y, self.t)

    def ydev(self, d):
        return (self.x * 4 + (self.y + d) % 4, self.t)

    def barrier(self, devs):
        b = pltpu.get_barrier_semaphore()
        for dev in devs:
            pl.semaphore_signal(b, inc=1, device_id=dev, device_id_type=MESH)
        pl.semaphore_wait(b, len(devs))

    def take(self, n=1):
        at = self.used
        self.used += n
        return at

    def copy(self, at, src, dst, dev):
        return pltpu.make_async_remote_copy(
            src_ref=src,
            dst_ref=dst,
            send_sem=self.send.at[at],
            recv_sem=self.recv.at[at],
            device_id=dev,
            device_id_type=MESH,
        )

    def go(self, src, dst, dev):
        copy = self.copy(self.take(), src, dst, dev)
        copy.start()
        return copy


HOPS = ("h1", "h2", "u1", "u2", "w1", "w2")


class ReduceZ:
    def __init__(self, k, part, rc, hp, hm, fp, fm):
        self.k, self.part, self.rc = k, part, rc
        self.hp, self.hm, self.fp, self.fm = hp, hm, fp, fm
        self.base = k.take(10)

    def _swap(self, d):
        k = self.k
        return k.copy(self.base + d, self.part.at[k.slot(d, 1 - k.c)], self.rc.at[d], k.sib())

    def swap(self, d):
        self._swap(d).start()

    def core_add(self, d):
        self._swap(d).wait_recv()
        mine = self.part.at[self.k.slot(d)]

        def body(i):
            s = rows(i, 32)
            mine[s] = mine[s] + self.rc[d, s]

        loop(4, body)

    def hop(self, name):
        k, p = self.k, self.part
        up, down = k.zdev(1), k.zdev(-1)
        src, dst, dev = {
            "h1": (p.at[k.slot(2), LO], self.hp, up),
            "h2": (p.at[k.slot(2), HI], self.hm, down),
            "u1": (p.at[k.slot(1), HI], self.fp.at[HI], up),
            "u2": (p.at[k.slot(3), LO], self.fm.at[LO], down),
            "w1": (p.at[k.slot(1), LO], self.fp.at[LO], up),
            "w2": (p.at[k.slot(3), HI], self.fm.at[HI], down),
        }[name]
        return k.copy(self.base + 4 + HOPS.index(name), src, dst, dev)

    def send(self, *names):
        for name in names:
            self.hop(name).start()

    def mid(self):
        k, p = self.k, self.part
        self.hop("h1").wait_recv()
        p[k.slot(1), LO] = p[k.slot(1), LO] + self.hp[...]
        self.send("w1")
        self.hop("h2").wait_recv()
        p[k.slot(3), HI] = p[k.slot(3), HI] + self.hm[...]
        self.send("w2")

    def finish(self):
        for name in ("u1", "u2", "w1", "w2"):
            self.hop(name).wait_recv()

    def own(self, s):
        mine = self.part[self.k.slot(0), s].astype(F32)
        return mine + self.fp[s].astype(F32) + self.fm[s].astype(F32)

    def drain(self):
        for d in range(4):
            self._swap(d).wait_send()
        for name in HOPS:
            self.hop(name).wait_send()


class GatherZ:
    def __init__(self, k, dst, own):
        self.k, self.dst, self.own = k, dst, own
        at = k.take(9)
        self.at = {name: at + i for i, name in enumerate(("a1", "b1", "a2", "b2", "s0", "f1", "f2", "s1", "s2"))}
        self.at["s3"] = k.take()

    def c(self, name):
        k, dst, own = self.k, self.dst, self.own
        me, below, above, far = k.t, k.slot(-1), k.slot(1), k.slot(2)
        up, down, sib = k.zdev(1), k.zdev(-1), k.sib()
        src, to, dev = {
            "a1": (own.at[LO], dst.at[me, LO], up),
            "b1": (own.at[HI], dst.at[me, HI], down),
            "a2": (own.at[HI], dst.at[me, HI], up),
            "b2": (own.at[LO], dst.at[me, LO], down),
            "s0": (own, dst.at[me], sib),
            "f1": (dst.at[below, LO], dst.at[below, LO], up),
            "f2": (dst.at[above, HI], dst.at[above, HI], down),
            "s1": (dst.at[below], dst.at[below], sib),
            "s2": (dst.at[above], dst.at[above], sib),
            "s3": (dst.at[far], dst.at[far], sib),
        }[name]
        return k.copy(self.at[name], src, to, dev)

    def start(self):
        for name in ("a1", "b1", "a2", "b2", "s0"):
            self.c(name).start()

    def forward(self):
        self.c("a1").wait_recv()
        self.c("f1").start()
        self.c("b1").wait_recv()
        self.c("f2").start()

    def share_near(self):
        self.c("b2").wait_recv()
        self.c("s2").start()
        self.c("a2").wait_recv()
        self.c("s1").start()

    def share_far(self):
        self.c("f1").wait_recv()
        self.c("f2").wait_recv()
        self.c("s3").start()

    def ready(self, d):
        self.c({0: "s0", 1: "s2", 3: "s1", 2: "s3"}[d]).wait_recv()

    def drain(self):
        for name in self.at:
            self.c(name).wait_send()


def ring4(k, view, hp, hm, fp, fm, dev, half, add, fin, sent):
    h1 = k.go(view(2, 0), hp, dev(1))
    h2 = k.go(view(2, 1), hm, dev(-1))
    u1 = k.go(view(1, 1), half(fp, 1), dev(1))
    u2 = k.go(view(3, 0), half(fm, 0), dev(-1))
    yield
    h1.wait_recv()
    add(view(1, 0), hp)
    w1 = k.go(view(1, 0), half(fp, 0), dev(1))
    h2.wait_recv()
    add(view(3, 1), hm)
    w2 = k.go(view(3, 1), half(fm, 1), dev(-1))
    sent.extend((h1, h2, u1, u2, w1, w2))
    yield
    for copy in (u1, w1, u2, w2):
        copy.wait_recv()
    fin()


def grads_xy(k, g, bufs, store, sent):
    R = g.shape[2]
    H, Q = R // 2, R // 4
    (hp1, hm1, fp1, fm1, hp2, hm2, fp2, fm2, tp1, tm1, tq1, tr1, tp2, tm2, tq2, tr2) = bufs
    first, second = pl.ds(0, H), pl.ds(H, H)

    def wide_half(f, h):
        return f.at[pl.ds(2 * h, 2)]

    def wide_add(dst, src):
        loop(2, lambda i: dst.__setitem__(i, dst[i] + src[i]))

    def wide_fin(own, fp, fm):
        def body(i):
            o = own(i)
            o[...] = (o[...].astype(F32) + fp[i].astype(F32) + fm[i].astype(F32)).astype(BF16)

        return lambda: loop(4, body)

    def thin_half(f, h):
        return f.at[pl.ds(Q * h, Q)]

    def thin_add(dst, src):
        dst[...] = dst[...] + src[...]

    a = ring4(
        k, lambda d, h: g.at[(k.x + d) % 4, pl.ds(2 * h, 2), first],
        hp1, hm1, fp1, fm1, k.xdev, wide_half, wide_add,
        wide_fin(lambda i: g.at[k.x, i, first], fp1, fm1), sent,
    )
    b = ring4(
        k, lambda d, h: g.at[pl.ds(2 * h, 2), (k.y + d) % 4, second],
        hp2, hm2, fp2, fm2, k.ydev, wide_half, wide_add,
        wide_fin(lambda i: g.at[i, k.y, second], fp2, fm2), sent,
    )
    next(a); next(b)
    yield
    next(a); next(b)
    yield
    for _ in a:
        pass
    for _ in b:
        pass

    def thin_fin(own, fp, fm, at):
        def fin():
            store(at, H, own[...].astype(F32) + fp[...].astype(F32) + fm[...].astype(F32))

        return fin

    a = ring4(
        k, lambda d, h: g.at[k.x, (k.y + d) % 4, pl.ds(Q * h, Q)],
        tp1, tm1, tq1, tr1, k.ydev, thin_half, thin_add,
        thin_fin(g.at[k.x, k.y, first], tq1, tr1, 0), sent,
    )
    b = ring4(
        k, lambda d, h: g.at[(k.x + d) % 4, k.y, pl.ds(H + Q * h, Q)],
        tp2, tm2, tq2, tr2, k.xdev, thin_half, thin_add,
        thin_fin(g.at[k.x, k.y, second], tq2, tr2, H), sent,
    )
    next(a); next(b)
    yield
    next(a); next(b)
    yield
    for _ in a:
        pass
    for _ in b:
        pass


def grads_bufs(R):
    H, Q = R // 2, R // 4
    b = lambda *s: pltpu.VMEM(s, BF16)
    wide = [b(2, H, 128), b(2, H, 128), b(4, H, 128), b(4, H, 128)]
    thin = [b(Q, 128), b(Q, 128), b(H, 128), b(H, 128)]
    return wide + wide + thin + thin


def unit(values):
    factor = lax.rsqrt(jnp.mean(values * values, axis=-1, keepdims=True) + EPSILON)
    return values * factor, factor


def norm_back(d_normed, gain, normed, factor):
    scaled = d_normed * gain
    return factor * (scaled - normed * jnp.mean(scaled * normed, axis=-1, keepdims=True))


def turn(values, cos, sin):
    return values * cos + pltpu.roll(values, 64, axis=1) * sin


NSEM = 256
NAMES = (
    "x", "oc", "wq", "wkv", "wo", "wg", "wu", "wd", "kvct", "cs", "gain1", "gain2", "lens", "out", "ig",
    "kvo", "gsum", "kvsum", "n1h", "ph", "XB", "N2", "OC", "PA", "PB", "RC", "hp", "hm", "fp", "fm",
    "hp2", "hm2", "fp2", "fm2", "h1", "dh1", "xs", "stage2", "wqkv", "wov", "q", "kv",
    "att", "dq", "dkv", "csv", "hid", "dg", "du", "gn", "kvb", "kvr", "kvi", "dkvs",
    "kvrc", "kvz", "kvx", "kvy", "kvct_v", "free_a", "free_b", "free_rc", "lsem", "send", "recv",
)


def rope_rows(lens, csv):
    low = lax.broadcasted_iota(jnp.int32, (1, 128), 1) < 64
    starts = [jnp.int32(0)]
    for doc in range(3):
        starts.append(starts[-1] + lens[0, doc])

    def look(i, found):
        s = rows(i, 256)
        place = lax.broadcasted_iota(jnp.int32, (256, 128), 0) + s.start
        table = csv[s, 0:128]
        return tuple(
            f + jnp.sum(jnp.where(place == start, table, 0.0), axis=0, keepdims=True)
            for f, start in zip(found, starts)
        )

    first = starts
    found = lax.fori_loop(0, 4, look, (jnp.zeros((1, 128), F32),) * 4)
    turned = [pltpu.roll(row, 64, axis=1) for row in found]
    a = [jnp.where(low, row, other) for row, other in zip(found, turned)]
    b = [jnp.where(low, other, -row) for row, other in zip(found, turned)]

    def body(i):
        s = rows(i, 256)
        place = lax.broadcasted_iota(jnp.int32, (256, 128), 0) + s.start
        here, aa, bb = jnp.zeros((256, 128), jnp.int32), a[0], b[0]
        for doc in (1, 2, 3):
            later = place >= first[doc]
            here = jnp.where(later, first[doc], here)
            aa = jnp.where(later, a[doc], aa)
            bb = jnp.where(later, b[doc], bb)
        table = csv[s, 0:128]
        both = table * aa + pltpu.roll(table, 64, axis=1) * bb
        other = pltpu.roll(both, 64, axis=1)
        csv[s, 0:128] = jnp.where(low, both, other)
        csv[s, 128:256] = jnp.where(low, -other, both)
        csv[s, 256:384] = here.astype(F32)

    loop(4, body)


def finish(out, ig, kvo, gsum, out_f, ig_f, kv_f, gq, go, gg, gu, gd, query, sem):
    copies = []

    def copy(src, dst):
        copies.append(pltpu.make_async_copy(src, dst, sem.at[len(copies)]))
        copies[-1].start()

    copy(gsum.at[pl.ds(2368, 256)], query)
    for i in range(4):
        s = pl.ds(256 * i, 256)
        copy(out.at[s], out_f.at[s])
        copy(ig.at[s], ig_f.at[s])
    copy(kvo, kv_f)
    copy(gsum.at[pl.ds(2112, 256)], go)
    copy(gsum.at[pl.ds(704, 704)], gg)
    copy(gsum.at[pl.ds(1408, 704)], gu)
    copy(gsum.at[pl.ds(0, 704)], gd)
    copies[0].wait()
    gq[...] = query[...].T
    for item in copies[1:]:
        item.wait()


def block(*refs):
    r = dict(zip(NAMES, refs))
    rest = refs[len(NAMES):]
    bufs_a, bufs_b = rest[0:16], rest[16:32]
    R = type("R", (), r)
    lsem = R.lsem
    k = Links(R.send, R.recv)
    XB, N2, OC, PA, PB = R.XB, R.N2, R.OC, R.PA, R.PB
    uses = [0]

    def local(src, dst):
        copy = pltpu.make_async_copy(src, dst, lsem.at[uses[0]])
        uses[0] += 1
        copy.start()
        return copy

    ld_x = local(R.x, XB)
    ld_q = local(R.wq, R.wqkv.at[:, pl.ds(0, 256)])
    ld_kv = local(R.wkv, R.wqkv.at[:, pl.ds(256, 256)])
    ld_cs = local(R.cs, R.csv.at[:, pl.ds(0, 128)])
    ld_wo = local(R.wo, R.wov)
    ld_oc = local(R.oc, OC)
    ld_ct = local(R.kvct.at[k.t], R.kvct_v)
    k.barrier(
        [k.zdev(1), k.zdev(-1), k.zdev(2), k.sib()]
        + [dev(d) for dev in (k.xdev, k.ydev) for d in (1, 2, 3)]
    )

    ld_x.wait()
    R.xs[...] = XB[k.t]

    def norm1(i):
        t, s = i // 2, rows(i % 2, 64)
        XB[t, s] = (unit(XB[t, s].astype(F32))[0] * R.gain1[...]).astype(BF16)

    loop(16, norm1)
    st_n1 = local(XB, R.n1h)
    ld_cs.wait()
    rope_rows(R.lens, R.csv)
    ld_q.wait()
    ld_kv.wait()

    def project(i):
        s = rows(i, 256)
        pre = dot(XB[pl.ds(2 * i, 2)].reshape(256, 2048), R.wqkv[...])
        cos, sin = R.csv[s, 0:128], R.csv[s, 128:256]
        for h in range(2):
            R.q[s, 128 * h:128 * h + 128] = turn(pre[:, 128 * h:128 * h + 128], cos, sin).astype(BF16)
        R.kv[s, 0:128] = turn(pre[:, 256:384], cos, sin).astype(BF16)
        R.kv[s, 128:256] = pre[:, 384:512].astype(BF16)

    loop(4, project)
    st_kv = local(R.kv, R.kvo)
    ld_wo.wait()

    def back_rows(j):
        return pl.ds(pl.multiple_of((j // 2) * (j - 2) * 256, 256), 768)

    rs = ReduceZ(k, PA, R.RC, R.hp, R.hm, R.fp, R.fm)

    def attend(i):
        d = (2 - i + 3 * (i // 2) - 2 * (i // 3)) % 4
        j = (k.z + d) % 4
        s, ks = rows(j, 256), back_rows(j)
        kk, vv = R.kv[ks, 0:128], R.kv[ks, 128:256]
        col = lax.broadcasted_iota(jnp.int32, (256, 768), 1) + ks.start
        row = lax.broadcasted_iota(jnp.int32, (256, 768), 0) + s.start
        first = R.csv[s, 256:384][:, 0:1].astype(jnp.int32)
        bias = jnp.where((col <= row) & (col >= first), 0.0, NEGATIVE)
        done = []
        for h in range(2):
            sc = dot(R.q[s, 128 * h:128 * h + 128], kk, NT) * SCALE + bias
            grown = jnp.exp(sc - jnp.max(sc, axis=-1, keepdims=True))
            probs = (grown * (1.0 / jnp.sum(grown, axis=-1, keepdims=True))).astype(BF16)
            PB[pl.ds(2 * j, 2), :, 768 * h:768 * h + 768] = probs.reshape(2, 128, 768)
            done.append(dot(probs, vv).astype(BF16))
        mixed = jnp.concatenate(done, axis=1)
        R.att[s] = mixed
        PA[pl.ds(2 * j, 2)] = dot(mixed, R.wov[...]).astype(BF16).reshape(2, 128, 2048)
        rs.swap(d)

        @pl.when(i == 1)
        def _():
            rs.core_add(2)
            rs.send("h1", "h2")

        @pl.when(i == 2)
        def _():
            rs.core_add(1)
            rs.send("u1")

        @pl.when(i == 3)
        def _():
            rs.core_add(3)
            rs.send("u2")

    loop(4, attend)
    st_p = local(PB.at[:, :, pl.ds(0, 1536)], R.ph)
    rs.core_add(0)
    rs.mid()
    g2 = GatherZ(k, N2, N2.at[k.t])
    dn = ReduceZ(k, PA, R.RC, R.hp, R.hm, R.fp, R.fm)
    ou = ReduceZ(k, PB, R.RC, R.hp2, R.hm2, R.fp2, R.fm2)
    gd = GatherZ(k, XB, XB.at[k.t])

    def mlp(wgv, wuv, wdv, wsem):
        lg = pltpu.make_async_copy(R.wg, wgv, wsem.at[0])
        lu = pltpu.make_async_copy(R.wu, wuv, wsem.at[1])
        ld = pltpu.make_async_copy(R.wd, wdv, wsem.at[2])
        ld.start()
        lg.start()
        lu.start()
        ld_oc.wait()
        ld.wait()

        def early(i):
            R.du[rows(i, 256)] = dot(OC[pl.ds(2 * i, 2)].reshape(256, 2048), wdv[...], NT).astype(BF16)

        loop(4, early)
        rs.finish()

        def shard1(i):
            s = rows(i, 32)
            h1 = R.xs[s].astype(F32) + rs.own(s)
            R.h1[s] = h1
            N2[k.t, s] = (unit(h1)[0] * R.gain2[...]).astype(BF16)

        loop(4, shard1)
        g2.start()
        rs.drain()
        lg.wait()
        lu.wait()
        st_n1.wait()
        st_p.wait()

        def chunk(i):
            d = i + i // 2 - 2 * (i // 3)
            j = (k.z + d) % 4
            s = rows(j, 256)

            @pl.when(i == 0)
            def _():
                g2.ready(0)

            @pl.when(i == 1)
            def _():
                g2.forward()
                g2.share_near()
                g2.ready(1)

            @pl.when(i == 2)
            def _():
                g2.ready(3)

            @pl.when(i == 3)
            def _():
                g2.share_far()
                g2.ready(2)

            n2 = N2[pl.ds(2 * j, 2)].reshape(256, 2048)
            gate = dot(n2, wgv[...], NT)
            up = dot(n2, wuv[...], NT)
            sig = 1.0 / (1.0 + jnp.exp(-gate))
            silu = gate * sig
            R.hid[s] = (silu * up).astype(BF16)
            dh = R.du[s].astype(F32)
            dg = (dh * up * sig * (1.0 + gate * (1.0 - sig))).astype(BF16)
            du = (dh * silu).astype(BF16)
            R.dg[s] = dg
            R.du[s] = du

            def cols(n):
                w = rows(n, 512)
                part = dot(R.dg[s], wgv[:, w]) + dot(R.du[s], wuv[:, w])
                PA[pl.ds(2 * j, 2), :, w] = part.astype(BF16).reshape(2, 128, 512)

            loop(4, cols)
            dn.swap(d)

            @pl.when(i == 1)
            def _():
                dn.core_add(0)

            @pl.when(i == 2)
            def _():
                dn.core_add(1)
                dn.send("u1")

            @pl.when(i == 3)
            def _():
                dn.core_add(3)
                dn.send("u2")

        loop(4, chunk)

        dn.core_add(2)
        dn.send("h1", "h2")

        def out_part(i):
            PB[pl.ds(2 * i, 2)] = dot(R.hid[rows(i, 256)], wdv[...]).astype(BF16).reshape(2, 128, 2048)

        loop(4, out_part)

    pl.run_scoped(
        mlp, b16(704, 2048), b16(704, 2048), b16(704, 2048),
        pltpu.SemaphoreType.DMA((3,)),
    )
    g2.drain()
    dn.mid()

    def weights(gm):
        sent_a, sent_b, sent_c, sent_d = [], [], [], []

        def grad(lhs, first, count, at, to, rhs):
            def body(n):
                left = lhs[:, first:first + count]
                res = dot(left, rhs[:, :, rows(n, 256)].reshape(1024, 256), TN).astype(BF16)
                for half in range(2):
                    e = 2 * n + half
                    at[e // 4, e % 4, to:to + count] = res[:, 128 * half:128 * half + 128]

            loop(8, body)

        def keep(offset):
            def store(at, count, value):
                R.gsum[offset + at:offset + at + count] = value

            return store

        grad(R.hid, 0, 704, gm.at[0], 0, OC)
        xy_down = grads_xy(k, gm.at[0], bufs_a, keep(0), sent_a)
        next(xy_down, None)
        ld_p = local(R.ph, OC.at[:, :, pl.ds(0, 1536)])
        dn.finish()
        R.gn[...] = jnp.zeros_like(R.gn)

        def shard2(i):
            s = rows(i, 32)
            d = dn.own(s)
            y2, r2 = unit(R.h1[s])
            dh1 = R.stage2[s].astype(F32) + norm_back(d, R.gain2[...], y2, r2)
            R.dh1[s] = dh1
            XB[k.t, s] = dh1.astype(BF16)
            dy = d * y2
            R.gn[0] += dy[0:8] + dy[8:16] + dy[16:24] + dy[24:32]

        loop(4, shard2)
        gd.start()
        dn.drain()
        grad(R.dg, 0, 704, gm.at[1], 0, N2)
        xy_gate = grads_xy(k, gm.at[1], bufs_b, keep(704), sent_b)
        next(xy_gate, None)
        next(xy_down, None)
        gd.ready(0)
        for d in range(4):
            ou.swap(d)
        gd.forward()
        grad(R.du, 0, 704, gm.at[2], 0, N2)
        for d in range(4):
            ou.core_add(d)
        ou.send("h1", "h2", "u1", "u2")
        pl.semaphore_signal(R.free_rc, inc=1, device_id=k.sib(), device_id_type=MESH)
        gd.share_near()
        next(xy_down, None)
        next(xy_gate, None)
        ld_p.wait()
        rn = ReduceZ(k, PA, R.RC, R.hp, R.hm, R.fp, R.fm)
        pl.semaphore_wait(R.free_rc, 1)
        R.dkv[...] = jnp.zeros_like(R.dkv)

        def back(i):
            d = i + i // 2 - 2 * (i // 3)
            j = (k.z + d) % 4
            s, ks = rows(j, 256), back_rows(j)

            @pl.when(i == 1)
            def _():
                gd.ready(1)

            @pl.when(i == 2)
            def _():
                gd.ready(3)

            @pl.when(i == 3)
            def _():
                gd.share_far()
                gd.ready(2)

            da = dot(XB[pl.ds(2 * j, 2)].reshape(256, 2048), R.wov[...], NT).astype(BF16)
            kk, vv = R.kv[ks, 0:128], R.kv[ks, 128:256]
            cos, sin = R.csv[s, 0:128], R.csv[s, 128:256]
            done = []
            for h in range(2):
                lanes = slice(128 * h, 128 * h + 128)
                probs = OC[pl.ds(2 * j, 2), :, 768 * h:768 * h + 768].reshape(256, 768)
                wide = probs.astype(F32)
                dp = dot(da[:, lanes], vv, NT)
                ds = (wide * (dp - jnp.sum(wide * dp, axis=-1, keepdims=True))).astype(BF16)
                done.append(turn(dot(ds, kk) * SCALE, cos, -sin).astype(BF16))
                R.dkv[ks, 0:128] += dot(ds, R.q[s, lanes], TN) * SCALE
                R.dkv[ks, 128:256] += dot(probs, da[:, lanes], TN)
            dq = jnp.concatenate(done, axis=1)
            R.dq[s] = dq
            PA[pl.ds(2 * j, 2)] = dot(dq, R.wqkv[:, 0:256], NT).astype(BF16).reshape(2, 128, 2048)
            rn.swap(d)

            @pl.when(i == 1)
            def _():
                rn.core_add(0)

            @pl.when(i == 2)
            def _():
                rn.core_add(1)
                rn.send("u1")

            @pl.when(i == 3)
            def _():
                rn.core_add(3)
                rn.send("u2")

        loop(4, back)
        rn.core_add(2)
        rn.send("h1", "h2")
        for d in range(4):
            for c in range(2):
                R.kvb[c, d] = R.dkv[(2 * d + c) * 128:(2 * d + c) * 128 + 128].astype(BF16)
        kv_swap = k.go(R.kvb.at[1 - k.c], R.kvr, k.sib())
        ld_n1 = local(R.n1h, OC)
        ou.mid()
        for _ in xy_down:
            pass
        next(xy_gate, None)

        def hand_over(sent, free):
            for dev in (k.xdev(1), k.xdev(-1), k.ydev(1), k.ydev(-1)):
                pl.semaphore_signal(free, inc=1, device_id=dev, device_id_type=MESH)
            for copy in sent:
                copy.wait_send()
            pl.semaphore_wait(free, 4)

        hand_over(sent_a, R.free_a)
        xy_up = grads_xy(k, gm.at[2], bufs_a, keep(1408), sent_c)
        next(xy_up, None)
        rn.mid()
        kv_swap.wait_recv()
        R.kvb[k.c] = R.kvb[k.c] + R.kvr[...]
        kv_in = [k.go(R.kvb.at[k.c, (k.z + d) % 4], R.kvi.at[d - 1], k.zdev(d)) for d in (1, 2, 3)]
        gat = gm.at[0, :, :, pl.ds(0, 512)]
        grad(R.att, 0, 256, gat, 0, XB)
        next(xy_gate, None)
        next(xy_up, None)
        ld_n1.wait()
        grad(R.dq, 0, 256, gat, 256, OC)
        for _ in xy_gate:
            pass
        hand_over(sent_b, R.free_b)

        def part(buf, n):
            return buf.at[:, pl.ds(0, n)] if len(buf.shape) == 3 else buf.at[pl.ds(0, n)]

        sizes = [256] * 8 + [128, 128, 256, 256] * 2
        bufs_c = [part(buf, n) for buf, n in zip(bufs_b, sizes)]
        xy_att = grads_xy(k, gat, bufs_c, keep(2112), sent_d)
        next(xy_att, None)
        next(xy_up, None)
        for copy in kv_in:
            copy.wait_recv()
        ld_ct.wait()
        total = R.kvb[k.c, k.z].astype(F32) + R.kvct_v[...]
        for d in range(3):
            total = total + R.kvi[d].astype(F32)
        own = rows(k.t, 128)
        cos, sin = R.csv[own, 0:128], R.csv[own, 128:256]
        R.dkvs[:, 0:128] = turn(total[:, 0:128], cos, -sin).astype(BF16)
        R.dkvs[:, 128:256] = total[:, 128:256].astype(BF16)
        rn.finish()
        gi = GatherZ(k, R.ig, R.xs)

        def shard3(i):
            s = rows(i, 32)
            d = rn.own(s) + dot(R.dkvs[s], R.wqkv[:, 256:512], NT)
            y1, r1 = unit(R.xs[s].astype(F32))
            R.xs[s] = (R.dh1[s] + norm_back(d, R.gain1[...], y1, r1)).astype(BF16)
            XB[k.t, s] = (y1 * R.gain1[...]).astype(BF16)
            dy = d * y1
            R.gn[1] += dy[0:8] + dy[8:16] + dy[16:24] + dy[24:32]

        gd.drain()
        R.gn[1] = jnp.zeros((8, 2048), F32)
        loop(4, shard3)
        gi.start()
        st_ig = local(R.xs, R.ig.at[k.t])
        ou.finish()

        def shard4(i):
            s = rows(i, 32)
            R.stage2[s] = (R.h1[s] + ou.own(s)).astype(BF16)

        loop(4, shard4)
        go = GatherZ(k, R.out, R.stage2)
        go.start()
        st_out = local(R.stage2, R.out.at[k.t])
        small = dot(XB[k.t], R.dkvs[...], TN)
        tops = [jnp.broadcast_to(jnp.sum(R.gn[i], axis=0, keepdims=True), (64, 2048)) for i in (1, 0)]
        small = jnp.concatenate([small, jnp.concatenate(tops, axis=0).T], axis=1).astype(BF16)
        sm = gm.at[1]
        for e in range(128):
            dp, at = e // 8, 48 * ((e % 2) * 4 + (e % 8) // 2)
            for n in range(3):
                sm[dp // 4, dp % 4, at + 16 * n:at + 16 * n + 16] = small[16 * e:16 * e + 16, 128 * n:128 * n + 128]
        sm_swap = k.go(sm.at[:, :, pl.ds(192 * (1 - k.c), 192)], R.kvrc, k.sib())
        next(xy_att, None)
        next(xy_up, None)
        gi.forward()
        sm_swap.wait_recv()
        for e in range(16):
            at = sm.at[e // 4, e % 4, pl.ds(192 * k.c, 192)]
            at[...] = at[...] + R.kvrc[e // 4, e % 4]
        mine = lambda d: sm.at[:, :, pl.ds(192 * k.c + 48 * ((k.z + d) % 4), 48)]
        z_in = [k.go(mine(d), R.kvz.at[d - 1], k.zdev(d)) for d in (1, 2, 3)]
        next(xy_att, None)
        next(xy_up, None)
        for copy in z_in:
            copy.wait_recv()
        R.kvz[3] = (mine(0)[...].astype(F32) + sum(R.kvz[i].astype(F32) for i in range(3))).astype(BF16)
        x_in = [k.go(R.kvz.at[3, (k.x + d) % 4], R.kvx.at[d - 1], k.xdev(d)) for d in (1, 2, 3)]
        gi.share_near()
        go.forward()
        go.share_near()
        for copy in x_in:
            copy.wait_recv()
        R.kvx[3] = (
            R.kvz[3, k.x].astype(F32) + sum(R.kvx[i].astype(F32) for i in range(3))
        ).astype(BF16)
        y_in = [k.go(R.kvx.at[3, (k.y + d) % 4], R.kvy.at[d - 1], k.ydev(d)) for d in (1, 2, 3)]
        next(xy_att, None)
        next(xy_up, None)
        for copy in y_in:
            copy.wait_recv()
        whole = R.kvx[3, k.y].astype(F32) + sum(R.kvy[i].astype(F32) for i in range(3))
        for n in range(3):
            R.kvsum[:, 128 * n:128 * n + 128] = whole[16 * n:16 * n + 16]
        gi.share_far()
        for xy in (xy_att, xy_up):
            for _ in xy:
                pass
        go.share_far()
        for ag in (gi, go):
            for d in (0, 1, 3, 2):
                ag.ready(d)
        for copy in sent_c + sent_d + kv_in + z_in + x_in + y_in + [kv_swap, sm_swap]:
            copy.wait_send()
        for item in (rn, ou, gi, go):
            item.drain()
        st_ig.wait()
        st_out.wait()

    R.stage2[...] = OC[k.t]
    pl.run_scoped(weights, pltpu.VMEM((3, 4, 4, 704, 128), BF16))
    st_kv.wait()


def b16(*s):
    return pltpu.VMEM(s, BF16)


def b32(*s):
    return pltpu.VMEM(s, F32)


def angle_table():
    inverse = np.exp(np.arange(64) * (-2.0 * math.log(10000.0) / 128))
    angle = np.arange(1024)[:, None] * inverse
    return np.concatenate([np.cos(angle), np.sin(angle)], axis=1).astype(np.float32)


def per_device(
    inputs, doc_lengths, norm1_gain, w_query, w_shared_kv, w_output, norm2_gain,
    w_gate, w_up, w_down, out_cotangent, kv_cotangent,
):
    cut = lambda v: v.reshape(8, 128, v.shape[-1])
    ins = [
        cut(inputs), cut(out_cotangent), w_query, w_shared_kv, w_output, w_gate.T, w_up.T, w_down,
        cut(kv_cotangent), jnp.asarray(angle_table()), norm1_gain.reshape(1, 2048), norm2_gain.reshape(1, 2048),
        doc_lengths,
    ]
    wide = ((8, 128, 2048), BF16)
    outs = [
        wide, wide, ((1024, 256), BF16), ((2624, 128), F32), ((16, 384), F32), wide, ((8, 128, 1536), BF16),
    ]
    big = b16(8, 128, 2048)
    hops = [b16(64, 2048), b16(64, 2048), b16(128, 2048), b16(128, 2048)]
    core = b16(4, 128, 2048)
    scratch = (
        [big] * 5 + [core] + hops + hops
        + [b32(128, 2048), b32(128, 2048), b16(128, 2048), b16(128, 2048)]
        + [b16(2048, 512), b16(256, 2048), b16(1024, 256), b16(1024, 256), b16(1024, 256), b16(1024, 256)]
        + [b32(1024, 256), b32(1024, 384), b16(1024, 704), b16(1024, 704), b16(1024, 704), b32(2, 8, 2048)]
        + [b16(2, 4, 128, 256), b16(4, 128, 256), b16(3, 128, 256), b16(128, 256)]
        + [b16(4, 4, 192, 128), b16(4, 4, 4, 48, 128), b16(4, 4, 48, 128), b16(3, 48, 128)]
        + [b32(128, 256), pltpu.SemaphoreType.REGULAR] + [pltpu.SemaphoreType.REGULAR] * 2 + [pltpu.SemaphoreType.DMA((16,))]
        + [pltpu.SemaphoreType.DMA((NSEM,)), pltpu.SemaphoreType.DMA((NSEM,))]
        + grads_bufs(704) + grads_bufs(704)
    )
    output, input_grad, shared_kv, gsum, kvsum, _, _ = pl.pallas_call(
        block,
        out_shape=[jax.ShapeDtypeStruct(s, d) for s, d in outs],
        in_specs=[ANY] * 10 + [VM] * 2 + [pl.BlockSpec(memory_space=pltpu.SMEM)],
        out_specs=[ANY] * 3 + [VM] * 2 + [ANY] * 2,
        scratch_shapes=scratch,
        compiler_params=pltpu.CompilerParams(
            collective_id=0, has_side_effects=True, vmem_limit_bytes=VLIM
        ),
    )(*ins)
    shapes = [
        ((1024, 2048), BF16), ((1024, 2048), BF16), ((1024, 256), BF16), ((128, 256), F32), ((256, 128), F32),
        ((704, 128), F32), ((704, 128), F32), ((704, 128), F32),
    ]
    flat = lambda v: v.reshape(1024, 2048)
    output, input_grad, shared_kv, g_query, g_out, g_gate, g_up, g_down = pl.pallas_call(
        finish,
        out_shape=[jax.ShapeDtypeStruct(s, d) for s, d in shapes],
        in_specs=[ANY] * 4,
        out_specs=[ANY] * 3 + [VM] + [ANY] * 4,
        scratch_shapes=[b32(256, 128), pltpu.SemaphoreType.DMA((14,))],
        compiler_params=pltpu.CompilerParams(vmem_limit_bytes=8 * 2**20),
    )(flat(output), flat(input_grad), shared_kv, gsum)
    return (
        output, input_grad, shared_kv, kvsum[:, 256], g_query, kvsum[:, 0:256], g_out, kvsum[:, 320],
        g_gate.T, g_up.T, g_down,
    )


VLIM = 63 * 2**20


def solution(mesh):
    placed = (
        P("dp", None), P("dp", None), P(), P(None, "tensor"), P(), P("tensor", None), P(),
        P(None, "tensor"), P(None, "tensor"), P("tensor", None), P("dp", None), P("dp", None),
    )
    return jax.shard_map(
        per_device,
        mesh=mesh,
        in_specs=placed,
        out_specs=(
            P("dp", None), P("dp", None), P("dp", None), P(("dp", "tensor")), P("dp", "tensor"),
            P(("dp", "tensor"), None), P("tensor", "dp"), P(("dp", "tensor")), P("dp", "tensor"),
            P("dp", "tensor"), P("tensor", "dp"),
        ),
        check_vma=False,
    )
```

```python
import math

import jax
import jax.numpy as jnp
import numpy as np
from jax import lax
from jax.experimental import pallas as pl
from jax.experimental.pallas import tpu as pltpu
from jax.sharding import PartitionSpec as P

EPSILON = 1e-05
NEGATIVE = -1e30
SCALE = 1.0 / math.sqrt(128)
MESH = pl.DeviceIdType.MESH
F32, BF16 = jnp.float32, jnp.bfloat16
VM = pl.BlockSpec(memory_space=pltpu.VMEM)
ANY = pl.BlockSpec(memory_space=pl.ANY)
NN, NT, TN = ((1,), (0,)), ((1,), (1,)), ((0,), (0,))
LO, HI = pl.ds(0, 64), pl.ds(64, 64)


def dot(a, b, dims=NN):
    return lax.dot_general(a, b, (dims, ((), ())), preferred_element_type=F32)


def loop(count, body):
    def one(i, carry):
        body(i)
        return carry

    lax.fori_loop(0, count, one, 0)


def rows(i, step):
    return pl.ds(pl.multiple_of(i * step, step), step)


class Links:
    def __init__(self, send, recv):
        dp, t = lax.axis_index("dp"), lax.axis_index("tensor")
        self.dp, self.t = dp, t
        self.x, self.y, self.z, self.c = dp // 4, dp % 4, t // 2, t % 2
        self.send, self.recv, self.used = send, recv, 0

    def slot(self, d, c=None):
        return 2 * ((self.z + d) % 4) + (self.c if c is None else c)

    def zdev(self, d):
        return (self.dp, self.slot(d))

    def sib(self):
        return (self.dp, self.slot(0, 1 - self.c))

    def xdev(self, d):
        return (((self.x + d) % 4) * 4 + self.y, self.t)

    def ydev(self, d):
        return (self.x * 4 + (self.y + d) % 4, self.t)

    def barrier(self, devs):
        b = pltpu.get_barrier_semaphore()
        for dev in devs:
            pl.semaphore_signal(b, inc=1, device_id=dev, device_id_type=MESH)
        pl.semaphore_wait(b, len(devs))

    def signal(self, sem, dev):
        pl.semaphore_signal(sem, inc=1, device_id=dev, device_id_type=MESH)

    def take(self, n=1):
        at = self.used
        self.used += n
        return at

    def copy(self, at, src, dst, dev):
        return pltpu.make_async_remote_copy(
            src_ref=src,
            dst_ref=dst,
            send_sem=self.send.at[at],
            recv_sem=self.recv.at[at],
            device_id=dev,
            device_id_type=MESH,
        )

    def go(self, src, dst, dev):
        copy = self.copy(self.take(), src, dst, dev)
        copy.start()
        return copy


HOPS = ("h1", "h2", "u1", "u2", "w1", "w2")


class ReduceZ:
    def __init__(self, k, part, rc, hp, hm, fp, fm):
        self.k, self.part, self.rc = k, part, rc
        self.hp, self.hm, self.fp, self.fm = hp, hm, fp, fm
        self.base = k.take(10)

    def _swap(self, d):
        k = self.k
        return k.copy(self.base + d, self.part.at[k.slot(d, 1 - k.c)], self.rc.at[d], k.sib())

    def swap(self, d):
        self._swap(d).start()

    def core_add(self, d):
        self._swap(d).wait_recv()
        mine = self.part.at[self.k.slot(d)]

        def body(i):
            s = rows(i, 32)
            mine[s] = mine[s] + self.rc[d, s]

        loop(4, body)

    def hop(self, name):
        k, p = self.k, self.part
        up, down = k.zdev(1), k.zdev(-1)
        src, dst, dev = {
            "h1": (p.at[k.slot(2), LO], self.hp, up),
            "h2": (p.at[k.slot(2), HI], self.hm, down),
            "u1": (p.at[k.slot(1), HI], self.fp.at[HI], up),
            "u2": (p.at[k.slot(3), LO], self.fm.at[LO], down),
            "w1": (p.at[k.slot(1), LO], self.fp.at[LO], up),
            "w2": (p.at[k.slot(3), HI], self.fm.at[HI], down),
        }[name]
        return k.copy(self.base + 4 + HOPS.index(name), src, dst, dev)

    def send(self, *names):
        for name in names:
            self.hop(name).start()

    def mid(self):
        k, p = self.k, self.part
        self.hop("h1").wait_recv()
        p[k.slot(1), LO] = p[k.slot(1), LO] + self.hp[...]
        self.send("w1")
        self.hop("h2").wait_recv()
        p[k.slot(3), HI] = p[k.slot(3), HI] + self.hm[...]
        self.send("w2")

    def finish(self):
        for name in ("u1", "u2", "w1", "w2"):
            self.hop(name).wait_recv()

    def own(self, s):
        mine = self.part[self.k.slot(0), s].astype(F32)
        return mine + self.fp[s].astype(F32) + self.fm[s].astype(F32)

    def drain(self):
        for d in range(4):
            self._swap(d).wait_send()
        for name in HOPS:
            self.hop(name).wait_send()


class GatherZ:
    def __init__(self, k, dst, own):
        self.k, self.dst, self.own = k, dst, own
        at = k.take(9)
        self.at = {name: at + i for i, name in enumerate(("a1", "b1", "a2", "b2", "s0", "f1", "f2", "s1", "s2"))}
        self.at["s3"] = k.take()

    def c(self, name):
        k, dst, own = self.k, self.dst, self.own
        me, below, above, far = k.t, k.slot(-1), k.slot(1), k.slot(2)
        up, down, sib = k.zdev(1), k.zdev(-1), k.sib()
        src, to, dev = {
            "a1": (own.at[LO], dst.at[me, LO], up),
            "b1": (own.at[HI], dst.at[me, HI], down),
            "a2": (own.at[HI], dst.at[me, HI], up),
            "b2": (own.at[LO], dst.at[me, LO], down),
            "s0": (own, dst.at[me], sib),
            "f1": (dst.at[below, LO], dst.at[below, LO], up),
            "f2": (dst.at[above, HI], dst.at[above, HI], down),
            "s1": (dst.at[below], dst.at[below], sib),
            "s2": (dst.at[above], dst.at[above], sib),
            "s3": (dst.at[far], dst.at[far], sib),
        }[name]
        return k.copy(self.at[name], src, to, dev)

    def start(self):
        for name in ("a1", "b1", "a2", "b2", "s0"):
            self.c(name).start()

    def forward(self):
        self.c("a1").wait_recv()
        self.c("f1").start()
        self.c("b1").wait_recv()
        self.c("f2").start()

    def share_near(self):
        self.c("b2").wait_recv()
        self.c("s2").start()
        self.c("a2").wait_recv()
        self.c("s1").start()

    def share_far(self):
        self.c("f1").wait_recv()
        self.c("f2").wait_recv()
        self.c("s3").start()

    def ready(self, d):
        self.c({0: "s0", 1: "s2", 3: "s1", 2: "s3"}[d]).wait_recv()

    def drain(self):
        for name in self.at:
            self.c(name).wait_send()


def ring4(k, view, hp, hm, fp, fm, dev, half, add, fin, sent):
    h1 = k.go(view(2, 0), hp, dev(1))
    h2 = k.go(view(2, 1), hm, dev(-1))
    u1 = k.go(view(1, 1), half(fp, 1), dev(1))
    u2 = k.go(view(3, 0), half(fm, 0), dev(-1))
    yield
    h1.wait_recv()
    add(view(1, 0), hp)
    w1 = k.go(view(1, 0), half(fp, 0), dev(1))
    h2.wait_recv()
    add(view(3, 1), hm)
    w2 = k.go(view(3, 1), half(fm, 1), dev(-1))
    sent.extend((h1, h2, u1, u2, w1, w2))
    yield
    for copy in (u1, w1, u2, w2):
        copy.wait_recv()
    fin()


def grads_xy(k, g, bufs, store, sent):
    R = g.shape[2]
    H, Q = R // 2, R // 4
    (hp1, hm1, fp1, fm1, hp2, hm2, fp2, fm2, tp1, tm1, tq1, tr1, tp2, tm2, tq2, tr2) = bufs
    first, second = pl.ds(0, H), pl.ds(H, H)

    def wide_half(f, h):
        return f.at[pl.ds(2 * h, 2)]

    def wide_add(dst, src):
        loop(2, lambda i: dst.__setitem__(i, dst[i] + src[i]))

    def wide_fin(own, fp, fm):
        def body(i):
            o = own(i)
            o[...] = (o[...].astype(F32) + fp[i].astype(F32) + fm[i].astype(F32)).astype(BF16)

        return lambda: loop(4, body)

    def thin_half(f, h):
        return f.at[pl.ds(Q * h, Q)]

    def thin_add(dst, src):
        dst[...] = dst[...] + src[...]

    a = ring4(
        k, lambda d, h: g.at[(k.x + d) % 4, pl.ds(2 * h, 2), first],
        hp1, hm1, fp1, fm1, k.xdev, wide_half, wide_add,
        wide_fin(lambda i: g.at[k.x, i, first], fp1, fm1), sent,
    )
    b = ring4(
        k, lambda d, h: g.at[pl.ds(2 * h, 2), (k.y + d) % 4, second],
        hp2, hm2, fp2, fm2, k.ydev, wide_half, wide_add,
        wide_fin(lambda i: g.at[i, k.y, second], fp2, fm2), sent,
    )
    next(a); next(b)
    yield
    next(a); next(b)
    yield
    for _ in a:
        pass
    for _ in b:
        pass

    def thin_fin(own, fp, fm, at):
        def fin():
            store(at, H, own[...].astype(F32) + fp[...].astype(F32) + fm[...].astype(F32))

        return fin

    a = ring4(
        k, lambda d, h: g.at[k.x, (k.y + d) % 4, pl.ds(Q * h, Q)],
        tp1, tm1, tq1, tr1, k.ydev, thin_half, thin_add,
        thin_fin(g.at[k.x, k.y, first], tq1, tr1, 0), sent,
    )
    b = ring4(
        k, lambda d, h: g.at[(k.x + d) % 4, k.y, pl.ds(H + Q * h, Q)],
        tp2, tm2, tq2, tr2, k.xdev, thin_half, thin_add,
        thin_fin(g.at[k.x, k.y, second], tq2, tr2, H), sent,
    )
    next(a); next(b)
    yield
    next(a); next(b)
    yield
    for _ in a:
        pass
    for _ in b:
        pass


def grads_bufs(R):
    H, Q = R // 2, R // 4
    b = lambda *s: pltpu.VMEM(s, BF16)
    wide = [b(2, H, 128), b(2, H, 128), b(4, H, 128), b(4, H, 128)]
    thin = [b(Q, 128), b(Q, 128), b(H, 128), b(H, 128)]
    return wide + wide + thin + thin


def unit(values):
    factor = lax.rsqrt(jnp.mean(values * values, axis=-1, keepdims=True) + EPSILON)
    return values * factor, factor


def norm_back(d_normed, gain, normed, factor):
    scaled = d_normed * gain
    return factor * (scaled - normed * jnp.mean(scaled * normed, axis=-1, keepdims=True))


def turn(values, cos, sin):
    return values * cos + pltpu.roll(values, 64, axis=1) * sin


NSEM = 256
NAMES = (
    "x", "oc", "wq", "wkv", "wo", "wg", "wu", "wd", "kvct", "cs", "gain1", "gain2", "lens", "out", "ig",
    "kvo", "gsum", "kvsum", "n1h", "ph", "XB", "N2", "OC", "PA", "PB", "RC", "hp", "hm", "fp", "fm",
    "hp2", "hm2", "fp2", "fm2", "h1", "dh1", "xs", "stage2", "wqkv", "wov", "q", "kv",
    "att", "dq", "dkv", "csv", "hid", "dg", "du", "gn", "kvb", "kvr", "kvi", "dkvs",
    "kvrc", "kvz", "kvs", "dkw", "kvx", "kvy", "kvct_v", "gst", "free_a", "free_b", "free_rc", "free_rn", "lsem", "send", "recv",
)


def rope_rows(lens, csv):
    low = lax.broadcasted_iota(jnp.int32, (1, 128), 1) < 64
    starts = [jnp.int32(0)]
    for doc in range(3):
        starts.append(starts[-1] + lens[0, doc])

    def look(i, found):
        s = rows(i, 256)
        place = lax.broadcasted_iota(jnp.int32, (256, 128), 0) + s.start
        table = csv[s, 0:128]
        return tuple(
            f + jnp.sum(jnp.where(place == start, table, 0.0), axis=0, keepdims=True)
            for f, start in zip(found, starts)
        )

    first = starts
    found = lax.fori_loop(0, 4, look, (jnp.zeros((1, 128), F32),) * 4)
    turned = [pltpu.roll(row, 64, axis=1) for row in found]
    a = [jnp.where(low, row, other) for row, other in zip(found, turned)]
    b = [jnp.where(low, other, -row) for row, other in zip(found, turned)]

    def body(i):
        s = rows(i, 256)
        place = lax.broadcasted_iota(jnp.int32, (256, 128), 0) + s.start
        here, aa, bb = jnp.zeros((256, 128), jnp.int32), a[0], b[0]
        for doc in (1, 2, 3):
            later = place >= first[doc]
            here = jnp.where(later, first[doc], here)
            aa = jnp.where(later, a[doc], aa)
            bb = jnp.where(later, b[doc], bb)
        table = csv[s, 0:128]
        both = table * aa + pltpu.roll(table, 64, axis=1) * bb
        csv[s, 0:128] = both
        csv[s, 128:256] = here.astype(F32)

    loop(4, body)


def cos_sin(csv, s):
    both = csv[s, 0:128]
    other = pltpu.roll(both, 64, axis=1)
    low = lax.broadcasted_iota(jnp.int32, both.shape, 1) < 64
    return jnp.where(low, both, other), jnp.where(low, -other, both)


def finish(out, ig, kvo, gsum, out_f, ig_f, kv_f, gq, go, gg, gu, gd, big, mid, small, sem):
    plan = []
    for i in range(4):
        s = pl.ds(256 * i, 256)
        plan.append((out.at[s], big.at[i], out_f.at[s]))
        plan.append((ig.at[s], big.at[4 + i], ig_f.at[s]))
    plan.append((kvo, mid, kv_f))
    for at, size, to in ((2112, 256, go), (704, 704, gg), (1408, 704, gu), (0, 704, gd)):
        plan.append((gsum.at[pl.ds(at, size)], small.at[pl.ds(at, size)], to))
    loads = [pltpu.make_async_copy(src, via, sem.at[0, n]) for n, (src, via, _) in enumerate(plan)]
    loads.append(pltpu.make_async_copy(gsum.at[pl.ds(2368, 256)], small.at[pl.ds(2368, 256)], sem.at[0, len(plan)]))
    for item in loads:
        item.start()
    stores = []
    for n, (_, via, dst) in enumerate(plan):
        loads[n].wait()
        stores.append(pltpu.make_async_copy(via, dst, sem.at[1, n]))
        stores[-1].start()
    loads[-1].wait()
    gq[...] = small[2368:2624].T
    for item in stores:
        item.wait()


def block(*refs):
    r = dict(zip(NAMES, refs))
    rest = refs[len(NAMES):]
    bufs_a, bufs_b = rest[0:16], rest[16:32]
    R = type("R", (), r)
    lsem = R.lsem
    k = Links(R.send, R.recv)
    XB, N2, OC, PA, PB = R.XB, R.N2, R.OC, R.PA, R.PB
    uses = [0]

    def local(src, dst):
        copy = pltpu.make_async_copy(src, dst, lsem.at[uses[0]])
        uses[0] += 1
        copy.start()
        return copy

    ld_x = local(R.x, XB)
    ld_q = local(R.wq, R.wqkv.at[:, pl.ds(0, 256)])
    ld_kv = local(R.wkv, R.wqkv.at[:, pl.ds(256, 256)])
    ld_cs = local(R.cs, R.csv.at[:, pl.ds(0, 128)])
    ld_wo = local(R.wo, R.wov)
    ld_oc = local(R.oc, OC)
    ld_ct = local(R.kvct.at[k.t], R.kvct_v)
    k.barrier(
        [k.zdev(1), k.zdev(-1), k.zdev(2), k.sib()]
        + [dev(d) for dev in (k.xdev, k.ydev) for d in (1, 2, 3)]
    )

    ld_x.wait()
    R.xs[...] = XB[k.t]

    def norm1(i):
        t, s = i // 2, rows(i % 2, 64)
        XB[t, s] = (unit(XB[t, s].astype(F32))[0] * R.gain1[...]).astype(BF16)

    loop(16, norm1)
    st_n1 = local(XB, R.n1h)
    ld_cs.wait()
    rope_rows(R.lens, R.csv)
    ld_q.wait()
    ld_kv.wait()

    def project(i):
        s = rows(i, 256)
        pre = dot(XB[pl.ds(2 * i, 2)].reshape(256, 2048), R.wqkv[...])
        cos, sin = cos_sin(R.csv, s)
        for h in range(2):
            R.q[s, 128 * h:128 * h + 128] = turn(pre[:, 128 * h:128 * h + 128], cos, sin).astype(BF16)
        R.kv[s, 0:128] = turn(pre[:, 256:384], cos, sin).astype(BF16)
        R.kv[s, 128:256] = pre[:, 384:512].astype(BF16)

    loop(4, project)
    st_kv = local(R.kv, R.kvo)
    ld_wo.wait()

    def back_rows(j):
        return pl.ds(pl.multiple_of((j // 2) * (j - 2) * 256, 256), 768)

    rs = ReduceZ(k, PA, R.RC, R.hp, R.hm, R.fp, R.fm)

    def attend(i):
        d = (2 - i + 3 * (i // 2) - 2 * (i // 3)) % 4
        j = (k.z + d) % 4
        s, ks = rows(j, 256), back_rows(j)
        kk, vv = R.kv[ks, 0:128], R.kv[ks, 128:256]
        col = lax.broadcasted_iota(jnp.int32, (256, 768), 1) + ks.start
        row = lax.broadcasted_iota(jnp.int32, (256, 768), 0) + s.start
        first = R.csv[s, 128:256][:, 0:1].astype(jnp.int32)
        bias = jnp.where((col <= row) & (col >= first), 0.0, NEGATIVE)
        done = []
        for h in range(2):
            sc = dot(R.q[s, 128 * h:128 * h + 128], kk, NT) * SCALE + bias
            grown = jnp.exp(sc - jnp.max(sc, axis=-1, keepdims=True))
            probs = (grown * (1.0 / jnp.sum(grown, axis=-1, keepdims=True))).astype(BF16)
            PB[pl.ds(2 * j, 2), :, 768 * h:768 * h + 768] = probs.reshape(2, 128, 768)
            done.append(dot(probs, vv).astype(BF16))
        mixed = jnp.concatenate(done, axis=1)
        R.att[s] = mixed
        PA[pl.ds(2 * j, 2)] = dot(mixed, R.wov[...]).astype(BF16).reshape(2, 128, 2048)
        rs.swap(d)

        @pl.when(i == 1)
        def _():
            rs.core_add(2)
            rs.send("h1", "h2")

        @pl.when(i == 2)
        def _():
            rs.core_add(1)
            rs.send("u1")

        @pl.when(i == 3)
        def _():
            rs.core_add(3)
            rs.send("u2")

    loop(4, attend)
    st_p = local(PB.at[:, :, pl.ds(0, 1536)], R.ph)
    rs.core_add(0)
    rs.mid()
    g2 = GatherZ(k, N2, N2.at[k.t])
    dn = ReduceZ(k, PA, R.RC, R.hp, R.hm, R.fp, R.fm)
    ou = ReduceZ(k, PB, R.RC, R.hp2, R.hm2, R.fp2, R.fm2)
    gd = GatherZ(k, XB, XB.at[k.t])

    def mlp(wgv, wuv, wdv, wsem):
        lg = pltpu.make_async_copy(R.wg, wgv, wsem.at[0])
        lu = pltpu.make_async_copy(R.wu, wuv, wsem.at[1])
        ld = pltpu.make_async_copy(R.wd, wdv, wsem.at[2])
        ld.start()
        lg.start()
        lu.start()
        ld_oc.wait()
        ld.wait()

        def early(i):
            R.du[rows(i, 256)] = dot(OC[pl.ds(2 * i, 2)].reshape(256, 2048), wdv[...], NT).astype(BF16)

        loop(4, early)
        rs.finish()

        def shard1(i):
            s = rows(i, 32)
            h1 = R.xs[s].astype(F32) + rs.own(s)
            R.h1[s] = h1
            N2[k.t, s] = (unit(h1)[0] * R.gain2[...]).astype(BF16)

        loop(4, shard1)
        g2.start()
        rs.drain()
        lg.wait()
        lu.wait()
        st_n1.wait()
        st_p.wait()

        def out_part(j):
            PB[pl.ds(2 * j, 2)] = dot(R.hid[rows(j, 256)], wdv[...]).astype(BF16).reshape(2, 128, 2048)

        def chunk(d):
            j = (k.z + d) % 4
            s = rows(j, 256)

            @pl.when(d == 0)
            def _():
                g2.ready(0)

            @pl.when(d == 1)
            def _():
                g2.forward()
                g2.share_near()
                g2.ready(1)

            @pl.when(d == 2)
            def _():
                g2.share_far()
                g2.ready(2)

            @pl.when(d == 3)
            def _():
                g2.ready(3)

            n2 = N2[pl.ds(2 * j, 2)].reshape(256, 2048)
            gate = dot(n2, wgv[...], NT)
            up = dot(n2, wuv[...], NT)
            sig = 1.0 / (1.0 + jnp.exp(-gate))
            silu = gate * sig
            R.hid[s] = (silu * up).astype(BF16)
            dh = R.du[s].astype(F32)
            dg = (dh * up * sig * (1.0 + gate * (1.0 - sig))).astype(BF16)
            du = (dh * silu).astype(BF16)
            R.dg[s] = dg
            R.du[s] = du

            @pl.when(d == 3)
            def _():
                dn.core_add(2)
                dn.send("h1", "h2")

            def cols(n):
                w = rows(n, 512)
                part = dot(R.dg[s], wgv[:, w]) + dot(R.du[s], wuv[:, w])
                PA[pl.ds(2 * j, 2), :, w] = part.astype(BF16).reshape(2, 128, 512)

            loop(4, cols)
            dn.swap(d)

            @pl.when(d < 2)
            def _():
                out_part(j)

            @pl.when(d == 1)
            def _():
                dn.core_add(0)

            @pl.when(d == 2)
            def _():
                dn.core_add(1)
                dn.send("u1")

        loop(4, chunk)

        out_part((k.z + 2) % 4)
        dn.core_add(3)
        dn.send("u2")
        k.signal(R.free_rc, k.sib())
        out_part((k.z + 3) % 4)

    pl.run_scoped(
        mlp, b16(704, 2048), b16(704, 2048), b16(704, 2048),
        pltpu.SemaphoreType.DMA((3,)),
    )
    g2.drain()
    dn.mid()
    pl.semaphore_wait(R.free_rc, 1)
    for d in range(4):
        ou.swap(d)

    def weights(gm):
        sent_a, sent_b, sent_c, sent_d = [], [], [], []

        def grad(lhs, first, count, at, to, rhs):
            def body(n):
                left = lhs[:, first:first + count]
                res = dot(left, rhs[:, :, rows(n, 256)].reshape(1024, 256), TN).astype(BF16)
                for half in range(2):
                    e = 2 * n + half
                    at[e // 4, e % 4, to:to + count] = res[:, 128 * half:128 * half + 128]

            loop(8, body)

        kept = {}

        def keep(offset):
            def store(at, count, value):
                slot = min(at, 1)
                if slot in kept:
                    kept[slot].wait()
                R.gst[slot, 0:count] = value
                kept[slot] = local(R.gst.at[slot, pl.ds(0, count)], R.gsum.at[pl.ds(offset + at, count)])

            return store

        grad(R.hid, 0, 704, gm.at[0], 0, OC)
        xy_down = grads_xy(k, gm.at[0], bufs_a, keep(0), sent_a)
        next(xy_down, None)
        ld_p = local(R.ph, OC.at[:, :, pl.ds(0, 1536)])
        for d in range(4):
            ou.core_add(d)
        ou.send("h1", "h2", "u1", "u2")
        k.signal(R.free_rn, k.sib())
        dn.finish()
        R.gn[...] = jnp.zeros_like(R.gn)

        def shard2(i):
            s = rows(i, 32)
            d = dn.own(s)
            y2, r2 = unit(R.h1[s])
            dh1 = R.stage2[s].astype(F32) + norm_back(d, R.gain2[...], y2, r2)
            R.dh1[s] = dh1
            XB[k.t, s] = dh1.astype(BF16)
            dy = d * y2
            R.gn[0] += dy[0:8] + dy[8:16] + dy[16:24] + dy[24:32]

        loop(4, shard2)
        gd.start()
        dn.drain()
        grad(R.dg, 0, 704, gm.at[1], 0, N2)
        xy_gate = grads_xy(k, gm.at[1], bufs_b, keep(704), sent_b)
        next(xy_gate, None)
        next(xy_down, None)
        ou.mid()
        gd.forward()
        grad(R.du, 0, 704, gm.at[2], 0, N2)
        R.dkv[...] = jnp.zeros_like(R.dkv)
        rn = ReduceZ(k, PA, R.RC, R.hp, R.hm, R.fp, R.fm)

        def back(d, between=None):
            j = (k.z + d) % 4
            s, ks = rows(j, 256), back_rows(j)
            da = dot(XB[pl.ds(2 * j, 2)].reshape(256, 2048), R.wov[...], NT).astype(BF16)
            kk, vv = R.kv[ks, 0:128], R.kv[ks, 128:256]
            cos, sin = cos_sin(R.csv, s)
            done = []
            for h in range(2):
                lanes = slice(128 * h, 128 * h + 128)
                probs = OC[pl.ds(2 * j, 2), :, 768 * h:768 * h + 768].reshape(256, 768)
                wide = probs.astype(F32)
                dp = dot(da[:, lanes], vv, NT)
                ds = (wide * (dp - jnp.sum(wide * dp, axis=-1, keepdims=True))).astype(BF16)
                done.append(turn(dot(ds, kk) * SCALE, cos, -sin).astype(BF16))
                R.dkv[ks, 0:128] += dot(ds, R.q[s, lanes], TN) * SCALE
                R.dkv[ks, 128:256] += dot(probs, da[:, lanes], TN)
            dq = jnp.concatenate(done, axis=1)
            R.dq[s] = dq
            if between:
                between()
            PA[pl.ds(2 * j, 2)] = dot(dq, R.wqkv[:, 0:256], NT).astype(BF16).reshape(2, 128, 2048)
            rn.swap(d)

        def shard4(i):
            s = rows(i, 32)
            R.stage2[s] = (R.h1[s] + ou.own(s)).astype(BF16)

        gd.ready(0)
        ld_p.wait()
        pl.semaphore_wait(R.free_rn, 1)
        back(0)
        gd.share_near()
        gd.ready(1)
        back(1)
        rn.core_add(0)
        next(xy_down, None)
        next(xy_gate, None)
        ou.finish()
        loop(4, shard4)
        go = GatherZ(k, R.out, R.stage2)
        go.start()
        st_out = local(R.stage2, R.out.at[k.t])
        gd.share_far()
        gd.ready(2)
        back(2)
        rn.core_add(1)
        rn.send("u1")
        gd.ready(3)

        def far():
            rn.core_add(2)
            rn.send("h1", "h2")

        back(3, far)
        for d in range(4):
            for c in range(2):
                R.kvb[c, d] = R.dkv[(2 * d + c) * 128:(2 * d + c) * 128 + 128].astype(BF16)
        kv_swap = k.go(R.kvb.at[1 - k.c], R.kvr, k.sib())
        ld_n1 = local(R.n1h, OC)
        rn.core_add(3)
        rn.send("u2")
        go.forward()
        for _ in xy_down:
            pass
        next(xy_gate, None)

        def hand_over(sent, free):
            for dev in (k.xdev(1), k.xdev(-1), k.ydev(1), k.ydev(-1)):
                k.signal(free, dev)
            for copy in sent:
                copy.wait_send()
            pl.semaphore_wait(free, 4)

        hand_over(sent_a, R.free_a)
        xy_up = grads_xy(k, gm.at[2], bufs_a, keep(1408), sent_c)
        next(xy_up, None)
        rn.mid()
        kv_swap.wait_recv()
        R.kvb[k.c] = R.kvb[k.c] + R.kvr[...]
        kv_in = [k.go(R.kvb.at[k.c, (k.z + d) % 4], R.kvi.at[d - 1], k.zdev(d)) for d in (1, 2, 3)]
        go.share_near()
        gat = gm.at[0, :, :, pl.ds(0, 512)]
        grad(R.att, 0, 256, gat, 0, XB)
        next(xy_gate, None)
        next(xy_up, None)
        go.share_far()
        ld_n1.wait()
        grad(R.dq, 0, 256, gat, 256, OC)
        for _ in xy_gate:
            pass
        hand_over(sent_b, R.free_b)

        def part(buf, n):
            return buf.at[:, pl.ds(0, n)] if len(buf.shape) == 3 else buf.at[pl.ds(0, n)]

        sizes = [256] * 8 + [128, 128, 256, 256] * 2
        bufs_c = [part(buf, n) for buf, n in zip(bufs_b, sizes)]
        xy_att = grads_xy(k, gat, bufs_c, keep(2112), sent_d)
        next(xy_att, None)
        next(xy_up, None)
        for copy in kv_in:
            copy.wait_recv()
        ld_ct.wait()
        total = R.kvb[k.c, k.z].astype(F32) + R.kvct_v[...]
        for d in range(3):
            total = total + R.kvi[d].astype(F32)
        own = rows(k.t, 128)
        cos, sin = cos_sin(R.csv, own)
        R.dkvs[:, 0:128] = turn(total[:, 0:128], cos, -sin).astype(BF16)
        R.dkvs[:, 128:256] = total[:, 128:256].astype(BF16)
        R.dkw[k.t] = R.dkvs[...]
        dk_in = [k.go(R.dkvs, R.dkw.at[k.t], k.zdev(d)) for d in (1, 2, 3)]
        dk_sib = [k.go(R.dkvs, R.dkw.at[k.t], k.sib())]
        rn.finish()
        gi = GatherZ(k, R.ig, R.xs)

        def shard3(i):
            s = rows(i, 32)
            d = rn.own(s) + dot(R.dkvs[s], R.wqkv[:, 256:512], NT)
            y1, r1 = unit(R.xs[s].astype(F32))
            R.xs[s] = (R.dh1[s] + norm_back(d, R.gain1[...], y1, r1)).astype(BF16)
            dy = d * y1
            R.gn[1] += dy[0:8] + dy[8:16] + dy[16:24] + dy[24:32]

        loop(4, shard3)
        gi.start()
        st_ig = local(R.xs, R.ig.at[k.t])
        sm = gm.at[1]
        tops = [jnp.broadcast_to(jnp.sum(R.gn[i], axis=0, keepdims=True), (64, 2048)) for i in (1, 0)]
        small = jnp.concatenate(tops, axis=0).T.astype(BF16)
        for e in range(128):
            dp, at = e // 8, 256 + 16 * ((e % 2) * 4 + (e % 8) // 2)
            sm[dp // 4, dp % 4, at:at + 16] = small[16 * e:16 * e + 16]
        sm_swap = k.go(sm.at[:, :, pl.ds(256 + 64 * (1 - k.c), 64)], R.kvrc, k.sib())
        for copy in dk_in:
            copy.wait_recv()
        dk_sib += [k.go(R.dkw.at[k.slot(d)], R.dkw.at[k.slot(d)], k.sib()) for d in (1, 2, 3)]
        next(xy_att, None)
        next(xy_up, None)
        for copy in dk_sib:
            copy.wait_recv()
        dkw = R.dkw[...].reshape(1024, 256)

        def grad_kv(n):
            res = dot(OC[:, :, rows(n, 256)].reshape(1024, 256), dkw, TN).astype(BF16)
            for e in range(16):
                dp = 2 * n + e // 8
                for half in range(2):
                    at = 32 * (e % 8) + 16 * half
                    sm[dp // 4, dp % 4, at:at + 16] = res[16 * e:16 * e + 16, 128 * half:128 * half + 128]

        loop(8, grad_kv)
        sm_swap.wait_recv()
        for e in range(16):
            at = sm.at[e // 4, e % 4, pl.ds(256 + 64 * k.c, 64)]
            at[...] = at[...] + R.kvrc[e // 4, e % 4]
        mine = lambda d: sm.at[:, :, pl.ds(256 + 64 * k.c + 16 * ((k.z + d) % 4), 16)]
        z_in = [k.go(mine(d), R.kvz.at[d - 1], k.zdev(d)) for d in (1, 2, 3)]
        next(xy_att, None)
        next(xy_up, None)
        gi.forward()
        for copy in z_in:
            copy.wait_recv()
        for e in range(16):
            q = (e // 4, e % 4)
            R.kvs[q[0], q[1], 0:32] = sm[q[0], q[1], pl.ds(32 * k.t, 32)]
            own = sm[q[0], q[1], pl.ds(256 + 64 * k.c + 16 * k.z, 16)].astype(F32)
            R.kvs[q[0], q[1], 32:48] = (own + sum(R.kvz[i, q[0], q[1]].astype(F32) for i in range(3))).astype(BF16)
        x_in = [k.go(R.kvs.at[(k.x + d) % 4], R.kvx.at[d - 1], k.xdev(d)) for d in (1, 2, 3)]
        gi.share_near()
        for copy in x_in:
            copy.wait_recv()
        R.kvx[3] = (R.kvs[k.x].astype(F32) + sum(R.kvx[i].astype(F32) for i in range(3))).astype(BF16)
        y_in = [k.go(R.kvx.at[3, (k.y + d) % 4], R.kvy.at[d - 1], k.ydev(d)) for d in (1, 2, 3)]
        next(xy_att, None)
        next(xy_up, None)
        for copy in y_in:
            copy.wait_recv()
        whole = R.kvx[3, k.y].astype(F32) + sum(R.kvy[i].astype(F32) for i in range(3))
        for n in range(3):
            R.kvsum[:, 128 * n:128 * n + 128] = whole[16 * n:16 * n + 16]
        for xy in (xy_att, xy_up):
            for _ in xy:
                pass
        gi.share_far()
        for ag in (go, gi):
            for d in (0, 1, 3, 2):
                ag.ready(d)
        for copy in sent_c + sent_d + kv_in + dk_in + dk_sib + z_in + x_in + y_in + [kv_swap, sm_swap]:
            copy.wait_send()
        for item in (gd, rn, ou, gi, go):
            item.drain()
        for copy in (st_ig, st_out, kept[0], kept[1]):
            copy.wait()

    R.stage2[...] = OC[k.t]
    pl.run_scoped(weights, pltpu.VMEM((3, 4, 4, 704, 128), BF16))
    st_kv.wait()


def b16(*s):
    return pltpu.VMEM(s, BF16)


def b32(*s):
    return pltpu.VMEM(s, F32)


def angle_table():
    inverse = np.exp(np.arange(64) * (-2.0 * math.log(10000.0) / 128))
    angle = np.arange(1024)[:, None] * inverse
    return np.concatenate([np.cos(angle), np.sin(angle)], axis=1).astype(np.float32)


def per_device(
    inputs, doc_lengths, norm1_gain, w_query, w_shared_kv, w_output, norm2_gain,
    w_gate, w_up, w_down, out_cotangent, kv_cotangent,
):
    cut = lambda v: v.reshape(8, 128, v.shape[-1])
    ins = [
        cut(inputs), cut(out_cotangent), w_query, w_shared_kv, w_output, w_gate.T, w_up.T, w_down,
        cut(kv_cotangent), jnp.asarray(angle_table()), norm1_gain.reshape(1, 2048), norm2_gain.reshape(1, 2048),
        doc_lengths,
    ]
    wide = ((8, 128, 2048), BF16)
    outs = [
        wide, wide, ((1024, 256), BF16), ((2624, 128), F32), ((16, 384), F32), wide, ((8, 128, 1536), BF16),
    ]
    big = b16(8, 128, 2048)
    hops = [b16(64, 2048), b16(64, 2048), b16(128, 2048), b16(128, 2048)]
    core = b16(4, 128, 2048)
    scratch = (
        [big] * 5 + [core] + hops + hops
        + [b32(128, 2048), b32(128, 2048), b16(128, 2048), b16(128, 2048)]
        + [b16(2048, 512), b16(256, 2048), b16(1024, 256), b16(1024, 256), b16(1024, 256), b16(1024, 256)]
        + [b32(1024, 256), b32(1024, 256), b16(1024, 704), b16(1024, 704), b16(1024, 704), b32(2, 8, 2048)]
        + [b16(2, 4, 128, 256), b16(4, 128, 256), b16(3, 128, 256), b16(128, 256)]
        + [b16(4, 4, 64, 128), b16(3, 4, 4, 16, 128), b16(4, 4, 48, 128), b16(8, 128, 256), b16(4, 4, 48, 128), b16(3, 48, 128)]
        + [b32(128, 256), b32(2, 352, 128), pltpu.SemaphoreType.REGULAR] + [pltpu.SemaphoreType.REGULAR] * 3 + [pltpu.SemaphoreType.DMA((24,))]
        + [pltpu.SemaphoreType.DMA((NSEM,)), pltpu.SemaphoreType.DMA((NSEM,))]
        + grads_bufs(704) + grads_bufs(704)
    )
    output, input_grad, shared_kv, gsum, kvsum, _, _ = pl.pallas_call(
        block,
        out_shape=[jax.ShapeDtypeStruct(s, d) for s, d in outs],
        in_specs=[ANY] * 10 + [VM] * 2 + [pl.BlockSpec(memory_space=pltpu.SMEM)],
        out_specs=[ANY] * 4 + [VM] + [ANY] * 2,
        scratch_shapes=scratch,
        compiler_params=pltpu.CompilerParams(
            collective_id=0, has_side_effects=True, vmem_limit_bytes=VLIM
        ),
    )(*ins)
    shapes = [
        ((1024, 2048), BF16), ((1024, 2048), BF16), ((1024, 256), BF16), ((128, 256), F32), ((256, 128), F32),
        ((704, 128), F32), ((704, 128), F32), ((704, 128), F32),
    ]
    flat = lambda v: v.reshape(1024, 2048)
    output, input_grad, shared_kv, g_query, g_out, g_gate, g_up, g_down = pl.pallas_call(
        finish,
        out_shape=[jax.ShapeDtypeStruct(s, d) for s, d in shapes],
        in_specs=[ANY] * 4,
        out_specs=[ANY] * 3 + [VM] + [ANY] * 4,
        scratch_shapes=[b16(8, 256, 2048), b16(1024, 256), b32(2624, 128), pltpu.SemaphoreType.DMA((2, 14))],
        compiler_params=pltpu.CompilerParams(vmem_limit_bytes=VLIM),
    )(flat(output), flat(input_grad), shared_kv, gsum)
    return (
        output, input_grad, shared_kv, kvsum[:, 256], g_query, kvsum[:, 0:256], g_out, kvsum[:, 320],
        g_gate.T, g_up.T, g_down,
    )


VLIM = 63 * 2**20 + 2**19


def solution(mesh):
    placed = (
        P("dp", None), P("dp", None), P(), P(None, "tensor"), P(), P("tensor", None), P(),
        P(None, "tensor"), P(None, "tensor"), P("tensor", None), P("dp", None), P("dp", None),
    )
    return jax.shard_map(
        per_device,
        mesh=mesh,
        in_specs=placed,
        out_specs=(
            P("dp", None), P("dp", None), P("dp", None), P(("dp", "tensor")), P("dp", "tensor"),
            P(("dp", "tensor"), None), P("tensor", "dp"), P(("dp", "tensor")), P("dp", "tensor"),
            P("dp", "tensor"), P("tensor", "dp"),
        ),
        check_vma=False,
    )
```

```python
import math

import jax
import jax.numpy as jnp
import numpy as np
from jax import lax
from jax.experimental import pallas as pl
from jax.experimental.pallas import tpu as pltpu
from jax.sharding import PartitionSpec as P

EPSILON = 1e-05
NEGATIVE = -1e30
SCALE = 1.0 / math.sqrt(128)
MESH = pl.DeviceIdType.MESH
F32, BF16 = jnp.float32, jnp.bfloat16
VM = pl.BlockSpec(memory_space=pltpu.VMEM)
ANY = pl.BlockSpec(memory_space=pl.ANY)
NN, NT, TN = ((1,), (0,)), ((1,), (1,)), ((0,), (0,))
LO, HI = pl.ds(0, 64), pl.ds(64, 64)


def dot(a, b, dims=NN):
    return lax.dot_general(a, b, (dims, ((), ())), preferred_element_type=F32)


def loop(count, body):
    def one(i, carry):
        body(i)
        return carry

    lax.fori_loop(0, count, one, 0)


def rows(i, step):
    return pl.ds(pl.multiple_of(i * step, step), step)


class Links:
    def __init__(self, send, recv):
        dp, t = lax.axis_index("dp"), lax.axis_index("tensor")
        self.dp, self.t = dp, t
        self.x, self.y, self.z, self.c = dp // 4, dp % 4, t // 2, t % 2
        self.send, self.recv, self.used = send, recv, 0

    def slot(self, d, c=None):
        return 2 * ((self.z + d) % 4) + (self.c if c is None else c)

    def zdev(self, d):
        return (self.dp, self.slot(d))

    def sib(self):
        return (self.dp, self.slot(0, 1 - self.c))

    def xdev(self, d):
        return (((self.x + d) % 4) * 4 + self.y, self.t)

    def ydev(self, d):
        return (self.x * 4 + (self.y + d) % 4, self.t)

    def greet(self, devs):
        b = pltpu.get_barrier_semaphore()
        for dev in devs:
            pl.semaphore_signal(b, inc=1, device_id=dev, device_id_type=MESH)
        return lambda: pl.semaphore_wait(b, len(devs))

    def signal(self, sem, dev):
        pl.semaphore_signal(sem, inc=1, device_id=dev, device_id_type=MESH)

    def take(self, n=1):
        at = self.used
        self.used += n
        return at

    def copy(self, at, src, dst, dev):
        return pltpu.make_async_remote_copy(
            src_ref=src,
            dst_ref=dst,
            send_sem=self.send.at[at],
            recv_sem=self.recv.at[at],
            device_id=dev,
            device_id_type=MESH,
        )

    def go(self, src, dst, dev):
        copy = self.copy(self.take(), src, dst, dev)
        copy.start()
        return copy


HOPS = ("h1", "h2", "u1", "u2", "w1", "w2")


class ReduceZ:
    def __init__(self, k, part, rc, hp, hm, fp, fm):
        self.k, self.part, (self.rc_to, self.rc_of) = k, part, rc
        self.hp, self.hm, self.fp, self.fm = hp, hm, fp, fm
        self.base = k.take(10)

    def _swap(self, d):
        k = self.k
        return k.copy(self.base + d, self.part.at[k.slot(d, 1 - k.c)], self.rc_to(d), k.sib())

    def swap(self, d):
        self._swap(d).start()

    def core_add(self, d):
        self._swap(d).wait_recv()
        mine, theirs = self.part.at[self.k.slot(d)], self.rc_of(d)

        def body(i):
            s = rows(i, 32)
            mine[s] = mine[s] + theirs[s]

        loop(4, body)

    def hop(self, name):
        k, p = self.k, self.part
        up, down = k.zdev(1), k.zdev(-1)
        src, dst, dev = {
            "h1": (p.at[k.slot(2), LO], self.hp, up),
            "h2": (p.at[k.slot(2), HI], self.hm, down),
            "u1": (p.at[k.slot(1), HI], self.fp.at[HI], up),
            "u2": (p.at[k.slot(3), LO], self.fm.at[LO], down),
            "w1": (p.at[k.slot(1), LO], self.fp.at[LO], up),
            "w2": (p.at[k.slot(3), HI], self.fm.at[HI], down),
        }[name]
        return k.copy(self.base + 4 + HOPS.index(name), src, dst, dev)

    def send(self, *names):
        for name in names:
            self.hop(name).start()

    def mid(self):
        k, p = self.k, self.part
        self.hop("h1").wait_recv()
        p[k.slot(1), LO] = p[k.slot(1), LO] + self.hp[...]
        self.send("w1")
        self.hop("h2").wait_recv()
        p[k.slot(3), HI] = p[k.slot(3), HI] + self.hm[...]
        self.send("w2")

    def finish(self):
        for name in ("u1", "u2", "w1", "w2"):
            self.hop(name).wait_recv()

    def own(self, s):
        mine = self.part[self.k.slot(0), s].astype(F32)
        return mine + self.fp[s].astype(F32) + self.fm[s].astype(F32)

    def drain(self):
        for d in range(4):
            self._swap(d).wait_send()
        for name in HOPS:
            self.hop(name).wait_send()


class GatherZ:
    def __init__(self, k, dst, own):
        self.k, self.dst, self.own = k, dst, own
        at = k.take(9)
        self.at = {name: at + i for i, name in enumerate(("a1", "b1", "a2", "b2", "s0", "f1", "f2", "s1", "s2"))}
        self.at["s3"] = k.take()

    def c(self, name):
        k, dst, own = self.k, self.dst, self.own
        me, below, above, far = k.t, k.slot(-1), k.slot(1), k.slot(2)
        up, down, sib = k.zdev(1), k.zdev(-1), k.sib()
        src, to, dev = {
            "a1": (own.at[LO], dst.at[me, LO], up),
            "b1": (own.at[HI], dst.at[me, HI], down),
            "a2": (own.at[HI], dst.at[me, HI], up),
            "b2": (own.at[LO], dst.at[me, LO], down),
            "s0": (own, dst.at[me], sib),
            "f1": (dst.at[below, LO], dst.at[below, LO], up),
            "f2": (dst.at[above, HI], dst.at[above, HI], down),
            "s1": (dst.at[below], dst.at[below], sib),
            "s2": (dst.at[above], dst.at[above], sib),
            "s3": (dst.at[far], dst.at[far], sib),
        }[name]
        return k.copy(self.at[name], src, to, dev)

    def start(self):
        for name in ("a1", "b1", "a2", "b2", "s0"):
            self.c(name).start()

    def forward(self):
        self.c("a1").wait_recv()
        self.c("f1").start()
        self.c("b1").wait_recv()
        self.c("f2").start()

    def share_near(self):
        self.c("b2").wait_recv()
        self.c("s2").start()
        self.c("a2").wait_recv()
        self.c("s1").start()

    def share_far(self):
        self.c("f1").wait_recv()
        self.c("f2").wait_recv()
        self.c("s3").start()

    def ready(self, d):
        self.c({0: "s0", 1: "s2", 3: "s1", 2: "s3"}[d]).wait_recv()

    def drain(self):
        for name in self.at:
            self.c(name).wait_send()


def ring4(k, view, hp, hm, fp, fm, dev, half, add, fin, sent):
    h1 = k.go(view(2, 0), hp, dev(1))
    h2 = k.go(view(2, 1), hm, dev(-1))
    u1 = k.go(view(1, 1), half(fp, 1), dev(1))
    u2 = k.go(view(3, 0), half(fm, 0), dev(-1))
    yield
    h1.wait_recv()
    add(view(1, 0), hp)
    w1 = k.go(view(1, 0), half(fp, 0), dev(1))
    h2.wait_recv()
    add(view(3, 1), hm)
    w2 = k.go(view(3, 1), half(fm, 1), dev(-1))
    sent.extend((h1, h2, u1, u2, w1, w2))
    yield
    for copy in (u1, w1, u2, w2):
        copy.wait_recv()
    fin()


def grads_xy(k, g, bufs, store, sent):
    R = g.shape[2]
    H, Q = R // 2, R // 4
    (hp1, hm1, fp1, fm1, hp2, hm2, fp2, fm2, tp1, tm1, tq1, tr1, tp2, tm2, tq2, tr2) = bufs
    first, second = pl.ds(0, H), pl.ds(H, H)

    def wide_half(f, h):
        return f.at[pl.ds(2 * h, 2)]

    def wide_add(dst, src):
        loop(2, lambda i: dst.__setitem__(i, dst[i] + src[i]))

    def wide_fin(own, fp, fm):
        def body(i):
            o = own(i)
            o[...] = (o[...].astype(F32) + fp[i].astype(F32) + fm[i].astype(F32)).astype(BF16)

        return lambda: loop(4, body)

    def thin_half(f, h):
        return f.at[pl.ds(Q * h, Q)]

    def thin_add(dst, src):
        dst[...] = dst[...] + src[...]

    a = ring4(
        k, lambda d, h: g.at[(k.x + d) % 4, pl.ds(2 * h, 2), first],
        hp1, hm1, fp1, fm1, k.xdev, wide_half, wide_add,
        wide_fin(lambda i: g.at[k.x, i, first], fp1, fm1), sent,
    )
    b = ring4(
        k, lambda d, h: g.at[pl.ds(2 * h, 2), (k.y + d) % 4, second],
        hp2, hm2, fp2, fm2, k.ydev, wide_half, wide_add,
        wide_fin(lambda i: g.at[i, k.y, second], fp2, fm2), sent,
    )
    next(a); next(b)
    yield
    next(a); next(b)
    yield
    for _ in a:
        pass
    for _ in b:
        pass

    def thin_fin(own, fp, fm, at):
        def fin():
            store(at, H, own[...].astype(F32) + fp[...].astype(F32) + fm[...].astype(F32))

        return fin

    a = ring4(
        k, lambda d, h: g.at[k.x, (k.y + d) % 4, pl.ds(Q * h, Q)],
        tp1, tm1, tq1, tr1, k.ydev, thin_half, thin_add,
        thin_fin(g.at[k.x, k.y, first], tq1, tr1, 0), sent,
    )
    b = ring4(
        k, lambda d, h: g.at[(k.x + d) % 4, k.y, pl.ds(H + Q * h, Q)],
        tp2, tm2, tq2, tr2, k.xdev, thin_half, thin_add,
        thin_fin(g.at[k.x, k.y, second], tq2, tr2, H), sent,
    )
    next(a); next(b)
    yield
    next(a); next(b)
    yield
    for _ in a:
        pass
    for _ in b:
        pass


def grads_bufs(R):
    H, Q = R // 2, R // 4
    b = lambda *s: pltpu.VMEM(s, BF16)
    wide = [b(2, H, 128), b(2, H, 128), b(4, H, 128), b(4, H, 128)]
    thin = [b(Q, 128), b(Q, 128), b(H, 128), b(H, 128)]
    return wide + wide + thin + thin


def unit(values):
    factor = lax.rsqrt(jnp.mean(values * values, axis=-1, keepdims=True) + EPSILON)
    return values * factor, factor


def norm_back(d_normed, gain, normed, factor):
    scaled = d_normed * gain
    return factor * (scaled - normed * jnp.mean(scaled * normed, axis=-1, keepdims=True))


def turn(values, cos, sin):
    return values * cos + pltpu.roll(values, 64, axis=1) * sin


NSEM = 256
NAMES = (
    "x", "oc", "wq", "wkv", "wo", "wg", "wu", "wd", "kvct", "cs", "gain1", "gain2", "lens", "out", "ig",
    "kvo", "gsum", "kvsum", "n1h", "ph", "wall", "XB", "N2", "OC", "PA", "PB", "RC", "hp", "hm", "fp", "fm",
    "hp2", "hm2", "fp2", "fm2", "h1", "dh1", "xs", "stage2", "wqkv", "wov", "q", "kv",
    "att", "dq", "dkv", "csv", "hid", "dg", "du", "gn", "kvb", "kvr", "kvi", "dkvs",
    "dqw", "kvx", "kvy", "nvx", "nvs", "nvy", "nvt", "nvr", "kvct_v", "gst", "free_a", "free_b",  "lsem", "send", "recv",
)


def rope_rows(lens, csv):
    low = lax.broadcasted_iota(jnp.int32, (1, 128), 1) < 64
    starts = [jnp.int32(0)]
    for doc in range(3):
        starts.append(starts[-1] + lens[0, doc])

    def look(i, found):
        s = rows(i, 256)
        place = lax.broadcasted_iota(jnp.int32, (256, 128), 0) + s.start
        table = csv[s, 0:128]
        return tuple(
            f + jnp.sum(jnp.where(place == start, table, 0.0), axis=0, keepdims=True)
            for f, start in zip(found, starts)
        )

    first = starts
    found = lax.fori_loop(0, 4, look, (jnp.zeros((1, 128), F32),) * 4)
    turned = [pltpu.roll(row, 64, axis=1) for row in found]
    a = [jnp.where(low, row, other) for row, other in zip(found, turned)]
    b = [jnp.where(low, other, -row) for row, other in zip(found, turned)]

    def body(i):
        s = rows(i, 256)
        place = lax.broadcasted_iota(jnp.int32, (256, 128), 0) + s.start
        here, aa, bb = jnp.zeros((256, 128), jnp.int32), a[0], b[0]
        for doc in (1, 2, 3):
            later = place >= first[doc]
            here = jnp.where(later, first[doc], here)
            aa = jnp.where(later, a[doc], aa)
            bb = jnp.where(later, b[doc], bb)
        table = csv[s, 0:128]
        both = table * aa + pltpu.roll(table, 64, axis=1) * bb
        csv[s, 0:128] = both
        csv[s, 128:256] = here.astype(F32)

    loop(4, body)


def cos_sin(csv, s):
    both = csv[s, 0:128]
    other = pltpu.roll(both, 64, axis=1)
    low = lax.broadcasted_iota(jnp.int32, both.shape, 1) < 64
    return jnp.where(low, both, other), jnp.where(low, -other, both)


def finish(out, ig, kvo, gsum, out_f, ig_f, kv_f, gq, go, gg, gu, gd, big, mid, small, sem):
    plan = []
    for i in range(4):
        s = pl.ds(256 * i, 256)
        plan.append((out.at[s], big.at[i], out_f.at[s]))
        plan.append((ig.at[s], big.at[4 + i], ig_f.at[s]))
    plan.append((kvo, mid, kv_f))
    for at, size, to in ((2112, 256, go), (704, 704, gg), (1408, 704, gu), (0, 704, gd)):
        plan.append((gsum.at[pl.ds(at, size)], small.at[pl.ds(at, size)], to))
    loads = [pltpu.make_async_copy(src, via, sem.at[0, n]) for n, (src, via, _) in enumerate(plan)]
    loads.append(pltpu.make_async_copy(gsum.at[pl.ds(2368, 256)], small.at[pl.ds(2368, 256)], sem.at[0, len(plan)]))
    for item in loads:
        item.start()
    stores = []
    for n, (_, via, dst) in enumerate(plan):
        loads[n].wait()
        stores.append(pltpu.make_async_copy(via, dst, sem.at[1, n]))
        stores[-1].start()
    loads[-1].wait()
    gq[...] = small[2368:2624].T
    for item in stores:
        item.wait()


def block(*refs):
    r = dict(zip(NAMES, refs))
    rest = refs[len(NAMES):]
    bufs_a, bufs_b = rest[0:16], rest[16:32]
    R = type("R", (), r)
    lsem = R.lsem
    k = Links(R.send, R.recv)
    XB, N2, OC, PA, PB = R.XB, R.N2, R.OC, R.PA, R.PB
    uses = [0]

    def local(src, dst):
        copy = pltpu.make_async_copy(src, dst, lsem.at[uses[0]])
        uses[0] += 1
        copy.start()
        return copy

    greeted = k.greet(
        [k.zdev(1), k.zdev(-1), k.zdev(2), k.sib()]
        + [(k.dp, k.slot(d, 1 - k.c)) for d in (1, 2, 3)]
        + [dev(d) for dev in (k.xdev, k.ydev) for d in (1, 2, 3)]
    )
    ld_q = local(R.wq, R.wqkv.at[:, pl.ds(0, 256)])
    ld_x = local(R.x, XB)
    ld_kv = local(R.wkv, R.wqkv.at[:, pl.ds(256, 256)])
    ld_cs = local(R.cs, R.csv.at[:, pl.ds(0, 128)])
    ld_wo = local(R.wo, R.wov)
    ld_oc = local(R.oc, OC)
    ld_ct = local(R.kvct.at[k.t], R.kvct_v)
    ld_q.wait()

    def turn_wq(i):
        s = rows(i, 256)
        PB[0:2, :, s] = R.wqkv[s, 0:256].T.reshape(2, 128, 256)

    loop(8, turn_wq)

    ld_x.wait()
    R.xs[...] = XB[k.t]

    def norm1(i):
        t, s = i // 2, rows(i % 2, 64)
        XB[t, s] = (unit(XB[t, s].astype(F32))[0] * R.gain1[...]).astype(BF16)

    loop(16, norm1)
    st_n1 = local(XB, R.n1h)
    greeted()
    W, half = R.wall, k.y // 2
    slim = pl.ds(pl.multiple_of(64 * (k.y % 2) + 16 * k.x, 16), 16)
    wide = pl.ds(pl.multiple_of(64 * (k.y % 2), 64), 64)
    w_z = [k.go(PB.at[half, slim], W.at[d, k.c, half, slim], k.zdev(-d)) for d in (1, 2, 3)]
    w_own = k.go(PB.at[pl.ds(0, 2)], W.at[0, k.c], k.sib())
    st_w = local(PB.at[pl.ds(0, 2)], W.at[0, k.c])
    ld_cs.wait()
    rope_rows(R.lens, R.csv)
    ld_kv.wait()

    def project(i):
        s = rows(i, 256)
        pre = dot(XB[pl.ds(2 * i, 2)].reshape(256, 2048), R.wqkv[...])
        cos, sin = cos_sin(R.csv, s)
        for h in range(2):
            R.q[s, 128 * h:128 * h + 128] = turn(pre[:, 128 * h:128 * h + 128], cos, sin).astype(BF16)
        R.kv[s, 0:128] = turn(pre[:, 256:384], cos, sin).astype(BF16)
        R.kv[s, 128:256] = pre[:, 384:512].astype(BF16)

    loop(4, project)
    st_kv = local(R.kv, R.kvo)
    ld_wo.wait()

    def back_rows(j):
        return pl.ds(pl.multiple_of((j // 2) * (j - 2) * 256, 256), 768)

    by_turn = (lambda d: R.RC.at[d],) * 2
    by_slot = (lambda d: XB.at[k.slot(d, 1 - k.c)], lambda d: XB.at[k.slot(d)])
    rs = ReduceZ(k, PA, by_turn, R.hp, R.hm, R.fp, R.fm)

    for copy in w_z:
        copy.wait_recv()
    near = W.at[pl.ds(1, 3), k.c, half, slim]
    w_x = [k.go(near, near, k.xdev(d)) for d in (1, 2, 3)]
    for copy in w_z + [w_own]:
        copy.wait_send()
    st_w.wait()

    def attend(i):
        d = (2 - i + 3 * (i // 2) - 2 * (i // 3)) % 4
        j = (k.z + d) % 4
        s, ks = rows(j, 256), back_rows(j)
        kk, vv = R.kv[ks, 0:128], R.kv[ks, 128:256]
        col = lax.broadcasted_iota(jnp.int32, (256, 768), 1) + ks.start
        row = lax.broadcasted_iota(jnp.int32, (256, 768), 0) + s.start
        first = R.csv[s, 128:256][:, 0:1].astype(jnp.int32)
        bias = jnp.where((col <= row) & (col >= first), 0.0, NEGATIVE)
        done = []
        for h in range(2):
            sc = dot(R.q[s, 128 * h:128 * h + 128], kk, NT) * SCALE + bias
            grown = jnp.exp(sc - jnp.max(sc, axis=-1, keepdims=True))
            probs = (grown * (1.0 / jnp.sum(grown, axis=-1, keepdims=True))).astype(BF16)
            PB[pl.ds(2 * j, 2), :, 768 * h:768 * h + 768] = probs.reshape(2, 128, 768)
            done.append(dot(probs, vv).astype(BF16))
        mixed = jnp.concatenate(done, axis=1)
        R.att[s] = mixed
        PA[pl.ds(2 * j, 2)] = dot(mixed, R.wov[...]).astype(BF16).reshape(2, 128, 2048)
        rs.swap(d)

        @pl.when(i == 1)
        def _():
            rs.core_add(2)
            rs.send("h1", "h2")

        @pl.when(i == 2)
        def _():
            rs.core_add(1)
            rs.send("u1")

        @pl.when(i == 3)
        def _():
            rs.core_add(3)
            rs.send("u2")

    loop(4, attend)
    st_p = local(PB.at[:, :, pl.ds(0, 1536)], R.ph)
    rs.core_add(0)
    rs.mid()
    for copy in w_x:
        copy.wait_recv()
    near = W.at[pl.ds(1, 3), k.c, half, wide]
    w_y = [k.go(near, near, k.ydev(d)) for d in (1, 2, 3)]
    g2 = GatherZ(k, N2, N2.at[k.t])
    dn = ReduceZ(k, PA, by_turn, R.hp, R.hm, R.fp, R.fm)
    ou = ReduceZ(k, PB, by_slot, R.hp2, R.hm2, R.fp2, R.fm2)
    gd = GatherZ(k, XB, XB.at[k.t])

    def mlp(wgv, wuv, wdv, wsem):
        lg = pltpu.make_async_copy(R.wg, wgv, wsem.at[0])
        lu = pltpu.make_async_copy(R.wu, wuv, wsem.at[1])
        ld = pltpu.make_async_copy(R.wd, wdv, wsem.at[2])
        ld.start()
        lg.start()
        lu.start()
        ld_oc.wait()
        ld.wait()

        def early(i):
            R.du[rows(i, 256)] = dot(OC[pl.ds(2 * i, 2)].reshape(256, 2048), wdv[...], NT).astype(BF16)

        loop(4, early)
        rs.finish()

        def shard1(i):
            s = rows(i, 32)
            h1 = R.xs[s].astype(F32) + rs.own(s)
            R.h1[s] = h1
            N2[k.t, s] = (unit(h1)[0] * R.gain2[...]).astype(BF16)

        loop(4, shard1)
        st_n1.wait()
        st_p.wait()
        g2.start()
        rs.drain()
        lg.wait()
        lu.wait()

        def out_part(j):
            PB[pl.ds(2 * j, 2)] = dot(R.hid[rows(j, 256)], wdv[...]).astype(BF16).reshape(2, 128, 2048)

        def chunk(d):
            j = (k.z + d) % 4
            s = rows(j, 256)

            @pl.when(d == 0)
            def _():
                g2.ready(0)

            @pl.when(d == 1)
            def _():
                g2.forward()
                g2.share_near()
                g2.ready(1)

            @pl.when(d == 2)
            def _():
                g2.share_far()
                g2.ready(2)

            @pl.when(d == 3)
            def _():
                g2.ready(3)

            n2 = N2[pl.ds(2 * j, 2)].reshape(256, 2048)
            gate = dot(n2, wgv[...], NT)
            up = dot(n2, wuv[...], NT)
            sig = 1.0 / (1.0 + jnp.exp(-gate))
            silu = gate * sig
            R.hid[s] = (silu * up).astype(BF16)
            dh = R.du[s].astype(F32)
            dg = (dh * up * sig * (1.0 + gate * (1.0 - sig))).astype(BF16)
            du = (dh * silu).astype(BF16)
            R.dg[s] = dg
            R.du[s] = du

            @pl.when(d == 3)
            def _():
                dn.core_add(2)
                dn.send("h1", "h2")

            def cols(n):
                w = rows(n, 512)
                part = dot(R.dg[s], wgv[:, w]) + dot(R.du[s], wuv[:, w])
                PA[pl.ds(2 * j, 2), :, w] = part.astype(BF16).reshape(2, 128, 512)

            loop(4, cols)
            dn.swap(d)

            out_part(j)
            ou.swap(d)

            @pl.when(d == 1)
            def _():
                dn.core_add(0)

            @pl.when(d == 2)
            def _():
                dn.core_add(1)
                dn.send("u1")
                ou.core_add(0)
                ou.core_add(1)
                ou.send("u1")

            @pl.when(d == 3)
            def _():
                ou.core_add(2)
                ou.send("h1", "h2")

        loop(4, chunk)
        dn.core_add(3)
        dn.send("u2")
        ou.core_add(3)
        ou.send("u2")

    pl.run_scoped(
        mlp, b16(704, 2048), b16(704, 2048), b16(704, 2048),
        pltpu.SemaphoreType.DMA((3,)),
    )
    g2.drain()
    dn.mid()
    for copy in w_y:
        copy.wait_recv()
    near = W.at[pl.ds(1, 3), k.c]
    w_core = k.go(near, near, k.sib())

    def weights(gm):
        sent_a, sent_b, sent_c, sent_d = [], [], [], []

        def grad(lhs, first, count, at, to, rhs):
            def body(n):
                left = lhs[:, first:first + count]
                res = dot(left, rhs[:, :, rows(n, 256)].reshape(1024, 256), TN).astype(BF16)
                for half in range(2):
                    e = 2 * n + half
                    at[e // 4, e % 4, to:to + count] = res[:, 128 * half:128 * half + 128]

            loop(8, body)

        kept = {}

        def keep(offset):
            def store(at, count, value):
                slot = min(at, 1)
                if slot in kept:
                    kept[slot].wait()
                R.gst[slot, 0:count] = value
                kept[slot] = local(R.gst.at[slot, pl.ds(0, count)], R.gsum.at[pl.ds(offset + at, count)])

            return store

        grad(R.hid, 0, 704, gm.at[0], 0, OC)
        xy_down = grads_xy(k, gm.at[0], bufs_a, keep(0), sent_a)
        next(xy_down, None)
        ld_p = local(R.ph, OC.at[:, :, pl.ds(0, 1536)])
        ou.mid()
        dn.finish()
        R.gn[...] = jnp.zeros_like(R.gn)

        def shard2(i):
            s = rows(i, 32)
            d = dn.own(s)
            y2, r2 = unit(R.h1[s])
            dh1 = R.stage2[s].astype(F32) + norm_back(d, R.gain2[...], y2, r2)
            R.dh1[s] = dh1
            XB[k.t, s] = dh1.astype(BF16)
            dy = d * y2
            R.gn[0] += dy[0:8] + dy[8:16] + dy[16:24] + dy[24:32]

        loop(4, shard2)
        gd.start()
        dn.drain()
        grad(R.dg, 0, 704, gm.at[1], 0, N2)
        xy_gate = grads_xy(k, gm.at[1], bufs_b, keep(704), sent_b)
        next(xy_gate, None)
        next(xy_down, None)
        ou.finish()

        def shard4(i):
            s = rows(i, 32)
            R.stage2[s] = (R.h1[s] + ou.own(s)).astype(BF16)

        loop(4, shard4)
        go = GatherZ(k, R.out, R.stage2)
        go.start()
        st_out = local(R.stage2, R.out.at[k.t])
        gd.forward()
        grad(R.du, 0, 704, gm.at[2], 0, N2)
        next(xy_down, None)
        next(xy_gate, None)
        w_own.wait_recv()
        w_core.wait_recv()

        def w_block(d, c):
            i = 2 * d + c
            return (PA if i < 4 else N2), pl.ds(2 * (i % 4), 2)

        ld_w = []
        for d in range(4):
            for c in range(2):
                buf, at = w_block(d, c)
                ld_w.append(local(W.at[d, c], buf.at[at]))
        R.dkv[...] = jnp.zeros_like(R.dkv)
        dq_in = []

        def back(d):
            j = (k.z + d) % 4
            s, ks = rows(j, 256), back_rows(j)
            da = dot(XB[pl.ds(2 * j, 2)].reshape(256, 2048), R.wov[...], NT).astype(BF16)
            kk, vv = R.kv[ks, 0:128], R.kv[ks, 128:256]
            cos, sin = cos_sin(R.csv, s)
            done = []
            for h in range(2):
                lanes = slice(128 * h, 128 * h + 128)
                probs = OC[pl.ds(2 * j, 2), :, 768 * h:768 * h + 768].reshape(256, 768)
                wide = probs.astype(F32)
                dp = dot(da[:, lanes], vv, NT)
                ds = (wide * (dp - jnp.sum(wide * dp, axis=-1, keepdims=True))).astype(BF16)
                done.append(turn(dot(ds, kk) * SCALE, cos, -sin).astype(BF16))
                R.dkv[ks, 0:128] += dot(ds, R.q[s, lanes], TN) * SCALE
                R.dkv[ks, 128:256] += dot(probs, da[:, lanes], TN)
            dq = jnp.concatenate(done, axis=1)
            R.dq[s] = dq
            for c in (k.c, 1 - k.c) if d else (1 - k.c,):
                to = k.slot(d, c)
                dq_in.append(k.go(R.dq.at[rows(to, 128)], R.dqw.at[k.t], (k.dp, to)))

        def give(free):
            for dev in (k.xdev(1), k.xdev(-1), k.ydev(1), k.ydev(-1)):
                k.signal(free, dev)

        gd.ready(0)
        ld_p.wait()
        back(0)
        gd.share_near()
        gd.ready(1)
        next(xy_down, None)
        next(xy_gate, None)
        back(1)
        for _ in xy_down:
            pass
        give(R.free_a)
        next(xy_gate, None)
        go.forward()
        gd.share_far()
        gd.ready(2)
        back(2)
        pl.semaphore_wait(R.free_a, 4)
        xy_up = grads_xy(k, gm.at[2], bufs_a, keep(1408), sent_c)
        next(xy_up, None)
        go.share_near()
        gd.ready(3)
        back(3)
        for d in range(4):
            for c in range(2):
                R.kvb[c, d] = R.dkv[(2 * d + c) * 128:(2 * d + c) * 128 + 128].astype(BF16)
        kv_swap = k.go(R.kvb.at[1 - k.c], R.kvr, k.sib())
        ld_n1 = local(R.n1h, OC)
        for _ in xy_gate:
            pass
        give(R.free_b)
        for copy in sent_a + sent_b:
            copy.wait_send()
        gat = gm.at[0, :, :, pl.ds(0, 512)]
        grad(R.att, 0, 256, gat, 0, XB)
        kv_swap.wait_recv()
        R.kvb[k.c] = R.kvb[k.c] + R.kvr[...]
        kv_in = [k.go(R.kvb.at[k.c, (k.z + d) % 4], R.kvi.at[d - 1], k.zdev(d)) for d in (1, 2, 3)]
        ld_n1.wait()
        grad(R.dq, 0, 256, gat, 256, OC)
        pl.semaphore_wait(R.free_b, 4)

        def part(buf, n):
            return buf.at[:, pl.ds(0, n)] if len(buf.shape) == 3 else buf.at[pl.ds(0, n)]

        sizes = [256] * 8 + [128, 128, 256, 256] * 2
        bufs_c = [part(buf, n) for buf, n in zip(bufs_b, sizes)]
        xy_att = grads_xy(k, gat, bufs_c, keep(2112), sent_d)
        next(xy_att, None)
        next(xy_up, None)
        R.dqw[k.t] = R.dq[rows(k.t, 128)]
        for copy in dq_in:
            copy.wait_recv()
        for copy in ld_w:
            copy.wait()

        def d_n1(n):
            w = rows(n, 512)
            total = jnp.zeros((128, 512), F32)
            for d in range(4):
                for c in range(2):
                    buf, at = w_block(d, c)
                    total = total + dot(R.dqw[k.slot(d, c)], buf[at, :, w].reshape(256, 512))
            R.h1[:, w] = total

        loop(4, d_n1)
        for copy in kv_in:
            copy.wait_recv()
        ld_ct.wait()
        total = R.kvb[k.c, k.z].astype(F32) + R.kvct_v[...]
        for d in range(3):
            total = total + R.kvi[d].astype(F32)
        own = rows(k.t, 128)
        cos, sin = cos_sin(R.csv, own)
        R.dkvs[:, 0:128] = turn(total[:, 0:128], cos, -sin).astype(BF16)
        R.dkvs[:, 128:256] = total[:, 128:256].astype(BF16)
        dkw = R.q
        dkw[own] = R.dkvs[...]
        dk_in = [k.go(R.dkvs, dkw.at[own], k.zdev(d)) for d in (1, 2, 3)]
        dk_sib = [k.go(R.dkvs, dkw.at[own], k.sib())]
        gi = GatherZ(k, R.ig, R.xs)

        def shard3(i):
            s = rows(i, 32)
            d = R.h1[s] + dot(R.dkvs[s], R.wqkv[:, 256:512], NT)
            y1, r1 = unit(R.xs[s].astype(F32))
            R.xs[s] = (R.dh1[s] + norm_back(d, R.gain1[...], y1, r1)).astype(BF16)
            dy = d * y1
            R.gn[1] += dy[0:8] + dy[8:16] + dy[16:24] + dy[24:32]

        loop(4, shard3)
        gi.start()
        st_ig = local(R.xs, R.ig.at[k.t])
        sm = gm.at[1]
        two = [jnp.sum(R.gn[i], axis=0, keepdims=True) for i in (1, 0)]
        two = jnp.concatenate(two + [jnp.zeros((14, 2048), F32)], axis=0).astype(BF16)
        for e in range(16):
            sm[e // 4, e % 4, 256:272] = two[:, 128 * e:128 * e + 128]
        line = pl.ds(256, 16)
        nx = [k.go(sm.at[(k.x + d) % 4, :, line], R.nvx.at[d - 1], k.xdev(d)) for d in (1, 2, 3)]
        for copy in dk_in:
            copy.wait_recv()
        theirs = [dkw.at[rows(k.slot(d), 128)] for d in (1, 2, 3)]
        dk_sib += [k.go(piece, piece, k.sib()) for piece in theirs]
        go.share_far()
        next(xy_att, None)
        next(xy_up, None)
        for copy in nx:
            copy.wait_recv()
        R.nvs[...] = (sm[k.x, :, line].astype(F32) + sum(R.nvx[i].astype(F32) for i in range(3))).astype(BF16)
        ny = [k.go(R.nvs.at[(k.y + d) % 4], R.nvy.at[d - 1], k.ydev(d)) for d in (1, 2, 3)]
        for copy in dk_sib:
            copy.wait_recv()

        def grad_kv(n):
            res = dot(OC[:, :, rows(n, 256)].reshape(1024, 256), dkw[...], TN).astype(BF16)
            for e in range(16):
                dp = 2 * n + e // 8
                for half in range(2):
                    at = 32 * (e % 8) + 16 * half
                    sm[dp // 4, dp % 4, at:at + 16] = res[16 * e:16 * e + 16, 128 * half:128 * half + 128]

        loop(8, grad_kv)
        mine = pl.ds(pl.multiple_of(32 * k.t, 32), 32)
        x_in = [k.go(sm.at[(k.x + d) % 4, :, mine], R.kvx.at[d - 1], k.xdev(d)) for d in (1, 2, 3)]
        for copy in ny:
            copy.wait_recv()
        R.nvt[...] = (R.nvs[k.y].astype(F32) + sum(R.nvy[i].astype(F32) for i in range(3))).astype(BF16)
        peers = [k.slot(d) for d in (1, 2, 3)] + [k.slot(d, 1 - k.c) for d in (0, 1, 2, 3)]
        nt = [k.go(R.nvt, R.nvr.at[i], (k.dp, peer)) for i, peer in enumerate(peers)]
        gi.forward()
        for copy in x_in:
            copy.wait_recv()
        R.kvx[3] = (sm[k.x, :, mine].astype(F32) + sum(R.kvx[i].astype(F32) for i in range(3))).astype(BF16)
        y_in = [k.go(R.kvx.at[3, (k.y + d) % 4], R.kvy.at[d - 1], k.ydev(d)) for d in (1, 2, 3)]
        next(xy_att, None)
        next(xy_up, None)
        gi.share_near()
        for copy in y_in + nt:
            copy.wait_recv()
        whole = R.kvx[3, k.y].astype(F32) + sum(R.kvy[i].astype(F32) for i in range(3))
        for n in range(2):
            R.kvsum[:, 128 * n:128 * n + 128] = whole[16 * n:16 * n + 16]
        gains = R.nvt[...].astype(F32) + sum(R.nvr[i].astype(F32) for i in range(7))
        R.kvsum[:, 256:384] = pltpu.roll(gains, (128 - 16 * k.t) % 128, axis=1)
        next(xy_att, None)
        for xy in (xy_att, xy_up):
            for _ in xy:
                pass
        gi.share_far()
        for ag in (go, gi):
            for d in (0, 1, 3, 2):
                ag.ready(d)
        for copy in w_x + w_y + [w_core] + sent_c + sent_d + dq_in + kv_in + dk_in + dk_sib + nx + ny + nt + x_in + y_in + [kv_swap]:
            copy.wait_send()
        for item in (gd, ou, gi, go):
            item.drain()
        for copy in (st_ig, st_out, kept[0], kept[1]):
            copy.wait()

    R.stage2[...] = OC[k.t]
    pl.run_scoped(weights, pltpu.VMEM((3, 4, 4, 704, 128), BF16))
    st_kv.wait()


def b16(*s):
    return pltpu.VMEM(s, BF16)


def b32(*s):
    return pltpu.VMEM(s, F32)


def angle_table():
    inverse = np.exp(np.arange(64) * (-2.0 * math.log(10000.0) / 128))
    angle = np.arange(1024)[:, None] * inverse
    return np.concatenate([np.cos(angle), np.sin(angle)], axis=1).astype(np.float32)


def per_device(
    inputs, doc_lengths, norm1_gain, w_query, w_shared_kv, w_output, norm2_gain,
    w_gate, w_up, w_down, out_cotangent, kv_cotangent,
):
    cut = lambda v: v.reshape(8, 128, v.shape[-1])
    ins = [
        cut(inputs), cut(out_cotangent), w_query, w_shared_kv, w_output, w_gate.T, w_up.T, w_down,
        cut(kv_cotangent), jnp.asarray(angle_table()), norm1_gain.reshape(1, 2048), norm2_gain.reshape(1, 2048),
        doc_lengths,
    ]
    wide = ((8, 128, 2048), BF16)
    outs = [
        wide, wide, ((1024, 256), BF16), ((2624, 128), F32), ((16, 384), F32), wide, ((8, 128, 1536), BF16),
        ((4, 2, 2, 128, 2048), BF16),
    ]
    big = b16(8, 128, 2048)
    hops = [b16(64, 2048), b16(64, 2048), b16(128, 2048), b16(128, 2048)]
    core = b16(4, 128, 2048)
    scratch = (
        [big] * 5 + [core] + hops + hops
        + [b32(128, 2048), b32(128, 2048), b16(128, 2048), b16(128, 2048)]
        + [b16(2048, 512), b16(256, 2048), b16(1024, 256), b16(1024, 256), b16(1024, 256), b16(1024, 256)]
        + [b32(1024, 256), b32(1024, 256), b16(1024, 704), b16(1024, 704), b16(1024, 704), b32(2, 8, 2048)]
        + [b16(2, 4, 128, 256), b16(4, 128, 256), b16(3, 128, 256), b16(128, 256)]
        + [b16(8, 128, 256), b16(4, 4, 32, 128), b16(3, 32, 128)]
        + [b16(3, 4, 16, 128), b16(4, 16, 128), b16(3, 16, 128), b16(16, 128), b16(7, 16, 128)]
        + [b32(128, 256), b32(2, 352, 128), pltpu.SemaphoreType.REGULAR] + [pltpu.SemaphoreType.REGULAR] + [pltpu.SemaphoreType.DMA((40,))]
        + [pltpu.SemaphoreType.DMA((NSEM,)), pltpu.SemaphoreType.DMA((NSEM,))]
        + grads_bufs(704) + grads_bufs(704)
    )
    output, input_grad, shared_kv, gsum, kvsum, *_ = pl.pallas_call(
        block,
        out_shape=[jax.ShapeDtypeStruct(s, d) for s, d in outs],
        in_specs=[ANY] * 10 + [VM] * 2 + [pl.BlockSpec(memory_space=pltpu.SMEM)],
        out_specs=[ANY] * 4 + [VM] + [ANY] * 3,
        scratch_shapes=scratch,
        compiler_params=pltpu.CompilerParams(
            collective_id=0, has_side_effects=True, vmem_limit_bytes=VLIM
        ),
    )(*ins)
    shapes = [
        ((1024, 2048), BF16), ((1024, 2048), BF16), ((1024, 256), BF16), ((128, 256), F32), ((256, 128), F32),
        ((704, 128), F32), ((704, 128), F32), ((704, 128), F32),
    ]
    flat = lambda v: v.reshape(1024, 2048)
    output, input_grad, shared_kv, g_query, g_out, g_gate, g_up, g_down = pl.pallas_call(
        finish,
        out_shape=[jax.ShapeDtypeStruct(s, d) for s, d in shapes],
        in_specs=[ANY] * 4,
        out_specs=[ANY] * 3 + [VM] + [ANY] * 4,
        scratch_shapes=[b16(8, 256, 2048), b16(1024, 256), b32(2624, 128), pltpu.SemaphoreType.DMA((2, 14))],
        compiler_params=pltpu.CompilerParams(vmem_limit_bytes=VLIM),
    )(flat(output), flat(input_grad), shared_kv, gsum)
    return (
        output, input_grad, shared_kv, kvsum[0, 256:272], g_query, kvsum[:, 0:256], g_out, kvsum[1, 256:272],
        g_gate.T, g_up.T, g_down,
    )


VLIM = 63 * 2**20 + 2**19


def solution(mesh):
    placed = (
        P("dp", None), P("dp", None), P(), P(None, "tensor"), P(), P("tensor", None), P(),
        P(None, "tensor"), P(None, "tensor"), P("tensor", None), P("dp", None), P("dp", None),
    )
    return jax.shard_map(
        per_device,
        mesh=mesh,
        in_specs=placed,
        out_specs=(
            P("dp", None), P("dp", None), P("dp", None), P(("dp", "tensor")), P("dp", "tensor"),
            P(("dp", "tensor"), None), P("tensor", "dp"), P(("dp", "tensor")), P("dp", "tensor"),
            P("dp", "tensor"), P("tensor", "dp"),
        ),
        check_vma=False,
    )
```

```python
import math

import jax
import jax.numpy as jnp
import numpy as np
from jax import lax
from jax.experimental import pallas as pl
from jax.experimental.pallas import tpu as pltpu
from jax.sharding import PartitionSpec as P

EPSILON = 1e-05
NEGATIVE = -1e30
SCALE = 1.0 / math.sqrt(128)
MESH = pl.DeviceIdType.MESH
F32, BF16 = jnp.float32, jnp.bfloat16
VM = pl.BlockSpec(memory_space=pltpu.VMEM)
ANY = pl.BlockSpec(memory_space=pl.ANY)
NN, NT, TN = ((1,), (0,)), ((1,), (1,)), ((0,), (0,))
LO, HI = pl.ds(0, 64), pl.ds(64, 64)


def dot(a, b, dims=NN):
    return lax.dot_general(a, b, (dims, ((), ())), preferred_element_type=F32)


def loop(count, body):
    def one(i, carry):
        body(i)
        return carry

    lax.fori_loop(0, count, one, 0)


def rows(i, step):
    return pl.ds(pl.multiple_of(i * step, step), step)


class Links:
    def __init__(self, send, recv):
        dp, t = lax.axis_index("dp"), lax.axis_index("tensor")
        self.dp, self.t = dp, t
        self.x, self.y, self.z, self.c = dp // 4, dp % 4, t // 2, t % 2
        self.send, self.recv, self.used = send, recv, 0

    def slot(self, d, c=None):
        return 2 * ((self.z + d) % 4) + (self.c if c is None else c)

    def zdev(self, d):
        return (self.dp, self.slot(d))

    def sib(self):
        return (self.dp, self.slot(0, 1 - self.c))

    def xdev(self, d):
        return (((self.x + d) % 4) * 4 + self.y, self.t)

    def ydev(self, d):
        return (self.x * 4 + (self.y + d) % 4, self.t)

    def greet(self, devs):
        b = pltpu.get_barrier_semaphore()
        for dev in devs:
            pl.semaphore_signal(b, inc=1, device_id=dev, device_id_type=MESH)
        return lambda: pl.semaphore_wait(b, len(devs))

    def signal(self, sem, dev):
        pl.semaphore_signal(sem, inc=1, device_id=dev, device_id_type=MESH)

    def take(self, n=1):
        at = self.used
        self.used += n
        return at

    def copy(self, at, src, dst, dev):
        return pltpu.make_async_remote_copy(
            src_ref=src,
            dst_ref=dst,
            send_sem=self.send.at[at],
            recv_sem=self.recv.at[at],
            device_id=dev,
            device_id_type=MESH,
        )

    def go(self, src, dst, dev):
        copy = self.copy(self.take(), src, dst, dev)
        copy.start()
        return copy


HOPS = ("h1", "h2", "u1", "u2", "w1", "w2")


class ReduceZ:
    def __init__(self, k, part, rc, hp, hm, fp, fm):
        self.k, self.part, (self.rc_to, self.rc_of) = k, part, rc
        self.hp, self.hm, self.fp, self.fm = hp, hm, fp, fm
        self.base = k.take(10)

    def _swap(self, d):
        k = self.k
        return k.copy(self.base + d, self.part.at[k.slot(d, 1 - k.c)], self.rc_to(d), k.sib())

    def swap(self, d):
        self._swap(d).start()

    def core_add(self, d):
        self._swap(d).wait_recv()
        mine, theirs = self.part.at[self.k.slot(d)], self.rc_of(d)

        def body(i):
            s = rows(i, 32)
            mine[s] = mine[s] + theirs[s]

        loop(4, body)

    def hop(self, name):
        k, p = self.k, self.part
        up, down = k.zdev(1), k.zdev(-1)
        src, dst, dev = {
            "h1": (p.at[k.slot(2), LO], self.hp, up),
            "h2": (p.at[k.slot(2), HI], self.hm, down),
            "u1": (p.at[k.slot(1), HI], self.fp.at[HI], up),
            "u2": (p.at[k.slot(3), LO], self.fm.at[LO], down),
            "w1": (p.at[k.slot(1), LO], self.fp.at[LO], up),
            "w2": (p.at[k.slot(3), HI], self.fm.at[HI], down),
        }[name]
        return k.copy(self.base + 4 + HOPS.index(name), src, dst, dev)

    def send(self, *names):
        for name in names:
            self.hop(name).start()

    def mid(self):
        k, p = self.k, self.part
        self.hop("h1").wait_recv()
        p[k.slot(1), LO] = p[k.slot(1), LO] + self.hp[...]
        self.send("w1")
        self.hop("h2").wait_recv()
        p[k.slot(3), HI] = p[k.slot(3), HI] + self.hm[...]
        self.send("w2")

    def finish(self):
        for name in ("u1", "u2", "w1", "w2"):
            self.hop(name).wait_recv()

    def own(self, s):
        mine = self.part[self.k.slot(0), s].astype(F32)
        return mine + self.fp[s].astype(F32) + self.fm[s].astype(F32)

    def drain(self):
        for d in range(4):
            self._swap(d).wait_send()
        for name in HOPS:
            self.hop(name).wait_send()


class GatherZ:
    def __init__(self, k, dst, own):
        self.k, self.dst, self.own = k, dst, own
        at = k.take(9)
        self.at = {name: at + i for i, name in enumerate(("a1", "b1", "a2", "b2", "s0", "f1", "f2", "s1", "s2"))}
        self.at["s3"] = k.take()

    def c(self, name):
        k, dst, own = self.k, self.dst, self.own
        me, below, above, far = k.t, k.slot(-1), k.slot(1), k.slot(2)
        up, down, sib = k.zdev(1), k.zdev(-1), k.sib()
        src, to, dev = {
            "a1": (own.at[LO], dst.at[me, LO], up),
            "b1": (own.at[HI], dst.at[me, HI], down),
            "a2": (own.at[HI], dst.at[me, HI], up),
            "b2": (own.at[LO], dst.at[me, LO], down),
            "s0": (own, dst.at[me], sib),
            "f1": (dst.at[below, LO], dst.at[below, LO], up),
            "f2": (dst.at[above, HI], dst.at[above, HI], down),
            "s1": (dst.at[below], dst.at[below], sib),
            "s2": (dst.at[above], dst.at[above], sib),
            "s3": (dst.at[far], dst.at[far], sib),
        }[name]
        return k.copy(self.at[name], src, to, dev)

    def start(self):
        for name in ("a1", "b1", "a2", "b2", "s0"):
            self.c(name).start()

    def forward(self):
        self.c("a1").wait_recv()
        self.c("f1").start()
        self.c("b1").wait_recv()
        self.c("f2").start()

    def share_near(self):
        self.c("b2").wait_recv()
        self.c("s2").start()
        self.c("a2").wait_recv()
        self.c("s1").start()

    def share_far(self):
        self.c("f1").wait_recv()
        self.c("f2").wait_recv()
        self.c("s3").start()

    def ready(self, d):
        self.c({0: "s0", 1: "s2", 3: "s1", 2: "s3"}[d]).wait_recv()

    def drain(self):
        for name in self.at:
            self.c(name).wait_send()


def ring4(k, view, hp, hm, fp, fm, dev, half, add, fin, sent):
    h1 = k.go(view(2, 0), hp, dev(1))
    h2 = k.go(view(2, 1), hm, dev(-1))
    u1 = k.go(view(1, 1), half(fp, 1), dev(1))
    u2 = k.go(view(3, 0), half(fm, 0), dev(-1))
    yield
    h1.wait_recv()
    add(view(1, 0), hp)
    w1 = k.go(view(1, 0), half(fp, 0), dev(1))
    h2.wait_recv()
    add(view(3, 1), hm)
    w2 = k.go(view(3, 1), half(fm, 1), dev(-1))
    sent.extend((h1, h2, u1, u2, w1, w2))
    yield
    for copy in (u1, w1, u2, w2):
        copy.wait_recv()
    fin()


def grads_xy(k, g, bufs, store, sent):
    R = g.shape[2]
    H, Q = R // 2, R // 4
    (hp1, hm1, fp1, fm1, hp2, hm2, fp2, fm2, tp1, tm1, tq1, tr1, tp2, tm2, tq2, tr2) = bufs
    first, second = pl.ds(0, H), pl.ds(H, H)

    def wide_half(f, h):
        return f.at[pl.ds(2 * h, 2)]

    def wide_add(dst, src):
        loop(2, lambda i: dst.__setitem__(i, dst[i] + src[i]))

    def wide_fin(own, fp, fm):
        def body(i):
            o = own(i)
            o[...] = (o[...].astype(F32) + fp[i].astype(F32) + fm[i].astype(F32)).astype(BF16)

        return lambda: loop(4, body)

    def thin_half(f, h):
        return f.at[pl.ds(Q * h, Q)]

    def thin_add(dst, src):
        dst[...] = dst[...] + src[...]

    a = ring4(
        k, lambda d, h: g.at[(k.x + d) % 4, pl.ds(2 * h, 2), first],
        hp1, hm1, fp1, fm1, k.xdev, wide_half, wide_add,
        wide_fin(lambda i: g.at[k.x, i, first], fp1, fm1), sent,
    )
    b = ring4(
        k, lambda d, h: g.at[pl.ds(2 * h, 2), (k.y + d) % 4, second],
        hp2, hm2, fp2, fm2, k.ydev, wide_half, wide_add,
        wide_fin(lambda i: g.at[i, k.y, second], fp2, fm2), sent,
    )
    next(a); next(b)
    yield
    next(a); next(b)
    yield
    for _ in a:
        pass
    for _ in b:
        pass

    def thin_fin(own, fp, fm, at):
        def fin():
            store(at, H, own[...].astype(F32) + fp[...].astype(F32) + fm[...].astype(F32))

        return fin

    a = ring4(
        k, lambda d, h: g.at[k.x, (k.y + d) % 4, pl.ds(Q * h, Q)],
        tp1, tm1, tq1, tr1, k.ydev, thin_half, thin_add,
        thin_fin(g.at[k.x, k.y, first], tq1, tr1, 0), sent,
    )
    b = ring4(
        k, lambda d, h: g.at[(k.x + d) % 4, k.y, pl.ds(H + Q * h, Q)],
        tp2, tm2, tq2, tr2, k.xdev, thin_half, thin_add,
        thin_fin(g.at[k.x, k.y, second], tq2, tr2, H), sent,
    )
    next(a); next(b)
    yield
    next(a); next(b)
    yield
    for _ in a:
        pass
    for _ in b:
        pass


def grads_bufs(R):
    H, Q = R // 2, R // 4
    b = lambda *s: pltpu.VMEM(s, BF16)
    wide = [b(2, H, 128), b(2, H, 128), b(4, H, 128), b(4, H, 128)]
    thin = [b(Q, 128), b(Q, 128), b(H, 128), b(H, 128)]
    return wide + wide + thin + thin


def unit(values):
    factor = lax.rsqrt(jnp.mean(values * values, axis=-1, keepdims=True) + EPSILON)
    return values * factor, factor


def norm_back(d_normed, gain, normed, factor):
    scaled = d_normed * gain
    return factor * (scaled - normed * jnp.mean(scaled * normed, axis=-1, keepdims=True))


def turn(values, cos, sin):
    return values * cos + pltpu.roll(values, 64, axis=1) * sin


NSEM = 256
NAMES = (
    "x", "oc", "wq", "wkv", "wo", "wg", "wu", "wd", "kvct", "cs", "gain1", "gain2", "lens", "out", "ig",
    "kvo", "gsum", "kvsum", "n1h", "ph", "wall", "XB", "N2", "OC", "PA", "PB", "RC", "hp", "hm", "fp", "fm",
    "hp2", "hm2", "fp2", "fm2", "h1", "dh1", "xs", "stage2", "wqkv", "wov", "q", "kv",
    "att", "dq", "dkv", "csv", "hid", "dg", "du", "gn", "kvb", "kvr", "kvi", "dkvs",
    "dqw", "kvx", "kvy", "nvx", "nvs", "nvy", "nvt", "nvr", "kvct_v", "gst", "free_a", "free_b",  "lsem", "send", "recv",
)


def rope_rows(lens, csv):
    low = lax.broadcasted_iota(jnp.int32, (1, 128), 1) < 64
    starts = [jnp.int32(0)]
    for doc in range(3):
        starts.append(starts[-1] + lens[0, doc])

    def look(i, found):
        s = rows(i, 256)
        place = lax.broadcasted_iota(jnp.int32, (256, 128), 0) + s.start
        table = csv[s, 0:128]
        return tuple(
            f + jnp.sum(jnp.where(place == start, table, 0.0), axis=0, keepdims=True)
            for f, start in zip(found, starts)
        )

    first = starts
    found = lax.fori_loop(0, 4, look, (jnp.zeros((1, 128), F32),) * 4)
    turned = [pltpu.roll(row, 64, axis=1) for row in found]
    a = [jnp.where(low, row, other) for row, other in zip(found, turned)]
    b = [jnp.where(low, other, -row) for row, other in zip(found, turned)]

    def body(i):
        s = rows(i, 256)
        place = lax.broadcasted_iota(jnp.int32, (256, 128), 0) + s.start
        here, aa, bb = jnp.zeros((256, 128), jnp.int32), a[0], b[0]
        for doc in (1, 2, 3):
            later = place >= first[doc]
            here = jnp.where(later, first[doc], here)
            aa = jnp.where(later, a[doc], aa)
            bb = jnp.where(later, b[doc], bb)
        table = csv[s, 0:128]
        both = table * aa + pltpu.roll(table, 64, axis=1) * bb
        csv[s, 0:128] = both
        csv[s, 128:256] = here.astype(F32)

    loop(4, body)


def cos_sin(csv, s):
    both = csv[s, 0:128]
    other = pltpu.roll(both, 64, axis=1)
    low = lax.broadcasted_iota(jnp.int32, both.shape, 1) < 64
    return jnp.where(low, both, other), jnp.where(low, -other, both)


def finish(out, ig, kvo, gsum, out_f, ig_f, kv_f, gq, go, gg, gu, gd, big, mid, small, sem):
    plan = []
    for i in range(4):
        s = pl.ds(256 * i, 256)
        plan.append((out.at[s], big.at[i], out_f.at[s]))
        plan.append((ig.at[s], big.at[4 + i], ig_f.at[s]))
    plan.append((kvo, mid, kv_f))
    for at, size, to in ((2112, 256, go), (704, 704, gg), (1408, 704, gu), (0, 704, gd)):
        plan.append((gsum.at[pl.ds(at, size)], small.at[pl.ds(at, size)], to))
    loads = [pltpu.make_async_copy(src, via, sem.at[0, n]) for n, (src, via, _) in enumerate(plan)]
    loads.append(pltpu.make_async_copy(gsum.at[pl.ds(2368, 256)], small.at[pl.ds(2368, 256)], sem.at[0, len(plan)]))
    for item in loads:
        item.start()
    stores = []
    for n, (_, via, dst) in enumerate(plan):
        loads[n].wait()
        stores.append(pltpu.make_async_copy(via, dst, sem.at[1, n]))
        stores[-1].start()
    loads[-1].wait()
    gq[...] = small[2368:2624].T
    for item in stores:
        item.wait()


def block(*refs):
    r = dict(zip(NAMES, refs))
    rest = refs[len(NAMES):]
    bufs_a, bufs_b = rest[0:16], rest[16:32]
    R = type("R", (), r)
    lsem = R.lsem
    k = Links(R.send, R.recv)
    XB, N2, OC, PA, PB = R.XB, R.N2, R.OC, R.PA, R.PB
    uses = [0]

    def local(src, dst):
        copy = pltpu.make_async_copy(src, dst, lsem.at[uses[0]])
        uses[0] += 1
        copy.start()
        return copy

    greeted = k.greet(
        [k.zdev(1), k.zdev(-1), k.zdev(2), k.sib()]
        + [(k.dp, k.slot(d, 1 - k.c)) for d in (1, 2, 3)]
        + [dev(d) for dev in (k.xdev, k.ydev) for d in (1, 2, 3)]
    )
    ld_cs = local(R.cs, R.csv.at[:, pl.ds(0, 128)])
    ld_q = local(R.wq, R.wqkv.at[:, pl.ds(0, 256)])
    quarter = [pl.ds(2 * i, 2) for i in range(4)]
    ld_x = [local(R.x.at[part], XB.at[part]) for part in quarter]
    ld_cs.wait()
    rope_rows(R.lens, R.csv)
    ld_q.wait()

    def turn_wq(i):
        s = rows(i, 256)
        PB[0:2, :, s] = R.wqkv[s, 0:256].T.reshape(2, 128, 256)

    loop(8, turn_wq)
    ld_ax = local(R.x.at[k.t], R.xs)

    def norm1(i):
        t, s = i // 2, rows(i % 2, 64)
        XB[t, s] = (unit(XB[t, s].astype(F32))[0] * R.gain1[...]).astype(BF16)

    for n in range(4):
        ld_x[n].wait()
        if n == 1:
            ld_kv = local(R.wkv, R.wqkv.at[:, pl.ds(256, 256)])
        loop(4, lambda i: norm1(4 * n + i))
    ld_wo = local(R.wo, R.wov)
    ld_oc = local(R.oc, OC)
    ld_ct = local(R.kvct.at[k.t], R.kvct_v)
    st_n1 = local(XB, R.n1h)
    greeted()
    W, half = R.wall, k.y // 2
    slim = pl.ds(pl.multiple_of(64 * (k.y % 2) + 16 * k.x, 16), 16)
    wide = pl.ds(pl.multiple_of(64 * (k.y % 2), 64), 64)
    w_z = [k.go(PB.at[half, slim], W.at[d, k.c, half, slim], k.zdev(-d)) for d in (1, 2, 3)]
    w_own = k.go(PB.at[pl.ds(0, 2)], W.at[0, k.c], k.sib())
    st_w = local(PB.at[pl.ds(0, 2)], W.at[0, k.c])
    ld_kv.wait()

    def project(i):
        s = rows(i, 256)
        pre = dot(XB[pl.ds(2 * i, 2)].reshape(256, 2048), R.wqkv[...])
        cos, sin = cos_sin(R.csv, s)
        for h in range(2):
            R.q[s, 128 * h:128 * h + 128] = turn(pre[:, 128 * h:128 * h + 128], cos, sin).astype(BF16)
        R.kv[s, 0:128] = turn(pre[:, 256:384], cos, sin).astype(BF16)
        R.kv[s, 128:256] = pre[:, 384:512].astype(BF16)

    loop(4, project)
    st_kv = local(R.kv, R.kvo)
    ld_wo.wait()

    def back_rows(j):
        return pl.ds(pl.multiple_of((j // 2) * (j - 2) * 256, 256), 768)

    by_turn = (lambda d: R.RC.at[d],) * 2
    by_slot = (lambda d: XB.at[k.slot(d, 1 - k.c)], lambda d: XB.at[k.slot(d)])
    rs = ReduceZ(k, PA, by_turn, R.hp, R.hm, R.fp, R.fm)

    for copy in w_z:
        copy.wait_recv()
    near = W.at[pl.ds(1, 3), k.c, half, slim]
    w_x = [k.go(near, near, k.xdev(d)) for d in (1, 2, 3)]
    for copy in w_z + [w_own]:
        copy.wait_send()
    st_w.wait()

    def attend(i):
        d = (2 - i + 3 * (i // 2) - 2 * (i // 3)) % 4
        j = (k.z + d) % 4
        s, ks = rows(j, 256), back_rows(j)
        kk, vv = R.kv[ks, 0:128], R.kv[ks, 128:256]
        col = lax.broadcasted_iota(jnp.int32, (256, 768), 1) + ks.start
        row = lax.broadcasted_iota(jnp.int32, (256, 768), 0) + s.start
        first = R.csv[s, 128:256][:, 0:1].astype(jnp.int32)
        bias = jnp.where((col <= row) & (col >= first), 0.0, NEGATIVE)
        done = []
        for h in range(2):
            sc = dot(R.q[s, 128 * h:128 * h + 128], kk, NT) * SCALE + bias
            grown = jnp.exp(sc - jnp.max(sc, axis=-1, keepdims=True))
            probs = (grown * (1.0 / jnp.sum(grown, axis=-1, keepdims=True))).astype(BF16)
            PB[pl.ds(2 * j, 2), :, 768 * h:768 * h + 768] = probs.reshape(2, 128, 768)
            done.append(dot(probs, vv).astype(BF16))
        mixed = jnp.concatenate(done, axis=1)
        R.att[s] = mixed
        PA[pl.ds(2 * j, 2)] = dot(mixed, R.wov[...]).astype(BF16).reshape(2, 128, 2048)
        rs.swap(d)

        @pl.when(i == 1)
        def _():
            rs.core_add(2)
            rs.send("h1", "h2")

        @pl.when(i == 2)
        def _():
            rs.core_add(1)
            rs.send("u1")

        @pl.when(i == 3)
        def _():
            rs.core_add(3)
            rs.send("u2")

    loop(4, attend)
    st_p = local(PB.at[:, :, pl.ds(0, 1536)], R.ph)
    rs.core_add(0)
    for copy in w_x:
        copy.wait_recv()
    near = W.at[pl.ds(1, 3), k.c, half, wide]
    w_y = [k.go(near, near, k.ydev(d)) for d in (1, 2, 3)]
    rs.mid()
    g2 = GatherZ(k, N2, N2.at[k.t])
    dn = ReduceZ(k, PA, by_turn, R.hp, R.hm, R.fp, R.fm)
    ou = ReduceZ(k, PB, by_slot, R.hp2, R.hm2, R.fp2, R.fm2)
    gd = GatherZ(k, XB, XB.at[k.t])

    def mlp(wgv, wuv, wdv, wsem):
        lg = pltpu.make_async_copy(R.wg, wgv, wsem.at[0])
        lu = pltpu.make_async_copy(R.wu, wuv, wsem.at[1])
        ld = pltpu.make_async_copy(R.wd, wdv, wsem.at[2])
        ld.start()
        lg.start()
        lu.start()
        ld_oc.wait()
        ld.wait()

        def early(i):
            R.du[rows(i, 256)] = dot(OC[pl.ds(2 * i, 2)].reshape(256, 2048), wdv[...], NT).astype(BF16)

        loop(4, early)
        rs.finish()
        ld_ax.wait()

        def shard1(i):
            s = rows(i, 32)
            h1 = R.xs[s].astype(F32) + rs.own(s)
            R.h1[s] = h1
            N2[k.t, s] = (unit(h1)[0] * R.gain2[...]).astype(BF16)

        loop(4, shard1)
        st_n1.wait()
        st_p.wait()
        g2.start()
        rs.drain()
        lg.wait()
        lu.wait()

        def out_part(j):
            PB[pl.ds(2 * j, 2)] = dot(R.hid[rows(j, 256)], wdv[...]).astype(BF16).reshape(2, 128, 2048)

        def chunk(d):
            j = (k.z + d) % 4
            s = rows(j, 256)

            @pl.when(d == 0)
            def _():
                g2.ready(0)

            @pl.when(d == 1)
            def _():
                g2.forward()
                g2.share_near()
                g2.ready(1)

            @pl.when(d == 2)
            def _():
                g2.share_far()
                g2.ready(2)

            @pl.when(d == 3)
            def _():
                g2.ready(3)

            n2 = N2[pl.ds(2 * j, 2)].reshape(256, 2048)
            gate = dot(n2, wgv[...], NT)
            up = dot(n2, wuv[...], NT)
            sig = 1.0 / (1.0 + jnp.exp(-gate))
            silu = gate * sig
            R.hid[s] = (silu * up).astype(BF16)
            dh = R.du[s].astype(F32)
            dg = (dh * up * sig * (1.0 + gate * (1.0 - sig))).astype(BF16)
            du = (dh * silu).astype(BF16)
            R.dg[s] = dg
            R.du[s] = du

            @pl.when(d == 2)
            def _():
                dn.core_add(1)
                dn.send("u1")
                ou.core_add(1)
                ou.send("u1")

            @pl.when(d == 3)
            def _():
                dn.core_add(2)
                dn.send("h1", "h2")
                ou.core_add(2)
                ou.send("h1", "h2")

            def cols(n):
                w = rows(n, 512)
                part = dot(R.dg[s], wgv[:, w]) + dot(R.du[s], wuv[:, w])
                PA[pl.ds(2 * j, 2), :, w] = part.astype(BF16).reshape(2, 128, 512)

            loop(4, cols)
            dn.swap(d)

            out_part(j)
            ou.swap(d)

            @pl.when(d == 1)
            def _():
                dn.core_add(0)
                ou.core_add(0)

        loop(4, chunk)
        dn.core_add(3)
        dn.send("u2")
        ou.core_add(3)
        ou.send("u2")

    pl.run_scoped(
        mlp, b16(704, 2048), b16(704, 2048), b16(704, 2048),
        pltpu.SemaphoreType.DMA((3,)),
    )
    g2.drain()
    dn.mid()

    def weights(gm):
        sent_a, sent_b, sent_c, sent_d = [], [], [], []

        def grad(lhs, first, count, at, to, rhs):
            def body(n):
                left = lhs[:, first:first + count]
                res = dot(left, rhs[:, :, rows(n, 256)].reshape(1024, 256), TN).astype(BF16)
                for half in range(2):
                    e = 2 * n + half
                    at[e // 4, e % 4, to:to + count] = res[:, 128 * half:128 * half + 128]

            loop(8, body)

        kept = {}

        def keep(offset):
            def store(at, count, value):
                slot = min(at, 1)
                if slot in kept:
                    kept[slot].wait()
                R.gst[slot, 0:count] = value
                kept[slot] = local(R.gst.at[slot, pl.ds(0, count)], R.gsum.at[pl.ds(offset + at, count)])

            return store

        grad(R.hid, 0, 704, gm.at[0], 0, OC)
        xy_down = grads_xy(k, gm.at[0], bufs_a, keep(0), sent_a)
        next(xy_down, None)
        ld_p = local(R.ph, OC.at[:, :, pl.ds(0, 1536)])
        ou.mid()
        grad(R.dg, 0, 704, gm.at[1], 0, N2)
        xy_gate = grads_xy(k, gm.at[1], bufs_b, keep(704), sent_b)
        next(xy_gate, None)
        dn.finish()
        R.gn[...] = jnp.zeros_like(R.gn)

        def shard2(i):
            s = rows(i, 32)
            d = dn.own(s)
            y2, r2 = unit(R.h1[s])
            dh1 = R.stage2[s].astype(F32) + norm_back(d, R.gain2[...], y2, r2)
            R.dh1[s] = dh1
            XB[k.t, s] = dh1.astype(BF16)
            dy = d * y2
            R.gn[0] += dy[0:8] + dy[8:16] + dy[16:24] + dy[24:32]

        loop(4, shard2)
        gd.start()
        dn.drain()
        for copy in w_y:
            copy.wait_recv()
        near = W.at[pl.ds(1, 3), k.c]
        w_core = k.go(near, near, k.sib())
        next(xy_down, None)
        ou.finish()

        def shard4(i):
            s = rows(i, 32)
            R.stage2[s] = (R.h1[s] + ou.own(s)).astype(BF16)

        loop(4, shard4)
        go = GatherZ(k, R.out, R.stage2)
        go.start()
        st_out = local(R.stage2, R.out.at[k.t])
        grad(R.du, 0, 704, gm.at[2], 0, N2)
        gd.forward()
        next(xy_down, None)
        next(xy_gate, None)
        R.dkv[...] = jnp.zeros_like(R.dkv)
        dq_in = []

        def back(d):
            j = (k.z + d) % 4
            s, ks = rows(j, 256), back_rows(j)
            da = dot(XB[pl.ds(2 * j, 2)].reshape(256, 2048), R.wov[...], NT).astype(BF16)
            kk, vv = R.kv[ks, 0:128], R.kv[ks, 128:256]
            cos, sin = cos_sin(R.csv, s)
            done = []
            for h in range(2):
                lanes = slice(128 * h, 128 * h + 128)
                probs = OC[pl.ds(2 * j, 2), :, 768 * h:768 * h + 768].reshape(256, 768)
                wide = probs.astype(F32)
                dp = dot(da[:, lanes], vv, NT)
                ds = (wide * (dp - jnp.sum(wide * dp, axis=-1, keepdims=True))).astype(BF16)
                done.append(turn(dot(ds, kk) * SCALE, cos, -sin).astype(BF16))
                R.dkv[ks, 0:128] += dot(ds, R.q[s, lanes], TN) * SCALE
                R.dkv[ks, 128:256] += dot(probs, da[:, lanes], TN)
            dq = jnp.concatenate(done, axis=1)
            R.dq[s] = dq
            for c in (k.c, 1 - k.c) if d else (1 - k.c,):
                to = k.slot(d, c)
                dq_in.append(k.go(R.dq.at[rows(to, 128)], R.dqw.at[k.t], (k.dp, to)))

        def give(free):
            for dev in (k.xdev(1), k.xdev(-1), k.ydev(1), k.ydev(-1)):
                k.signal(free, dev)

        gd.ready(0)
        ld_p.wait()
        back(0)
        gd.share_near()
        gd.ready(1)
        next(xy_down, None)
        next(xy_gate, None)
        w_own.wait_recv()
        w_core.wait_recv()

        def w_block(d, c):
            i = 2 * d + c
            return (PA if i < 4 else N2), pl.ds(2 * (i % 4), 2)

        ld_w = []
        for d in range(4):
            for c in range(2):
                buf, at = w_block(d, c)
                ld_w.append(local(W.at[d, c], buf.at[at]))
        back(1)
        for _ in xy_down:
            pass
        give(R.free_a)
        next(xy_gate, None)
        gd.ready(3)
        back(3)
        go.forward()
        gd.share_far()
        pl.semaphore_wait(R.free_a, 4)
        xy_up = grads_xy(k, gm.at[2], bufs_a, keep(1408), sent_c)
        next(xy_up, None)
        gd.ready(2)
        back(2)
        go.share_near()
        for d in range(4):
            for c in range(2):
                R.kvb[c, d] = R.dkv[(2 * d + c) * 128:(2 * d + c) * 128 + 128].astype(BF16)
        kv_swap = k.go(R.kvb.at[1 - k.c], R.kvr, k.sib())
        ld_n1 = local(R.n1h, OC)
        for _ in xy_gate:
            pass
        give(R.free_b)
        for copy in sent_a + sent_b:
            copy.wait_send()
        gat = gm.at[0, :, :, pl.ds(0, 512)]
        grad(R.att, 0, 256, gat, 0, XB)
        kv_swap.wait_recv()
        R.kvb[k.c] = R.kvb[k.c] + R.kvr[...]
        kv_in = [k.go(R.kvb.at[k.c, (k.z + d) % 4], R.kvi.at[d - 1], k.zdev(d)) for d in (1, 2, 3)]
        ld_n1.wait()
        grad(R.dq, 0, 256, gat, 256, OC)
        pl.semaphore_wait(R.free_b, 4)

        def part(buf, n):
            return buf.at[:, pl.ds(0, n)] if len(buf.shape) == 3 else buf.at[pl.ds(0, n)]

        sizes = [256] * 8 + [128, 128, 256, 256] * 2
        bufs_c = [part(buf, n) for buf, n in zip(bufs_b, sizes)]
        xy_att = grads_xy(k, gat, bufs_c, keep(2112), sent_d)
        next(xy_att, None)
        next(xy_up, None)
        R.dqw[k.t] = R.dq[rows(k.t, 128)]
        for copy in dq_in:
            copy.wait_recv()
        for copy in ld_w:
            copy.wait()

        def d_n1(n):
            w = rows(n, 512)
            total = jnp.zeros((128, 512), F32)
            for d in range(4):
                for c in range(2):
                    buf, at = w_block(d, c)
                    total = total + dot(R.dqw[k.slot(d, c)], buf[at, :, w].reshape(256, 512))
            R.h1[:, w] = total

        loop(4, d_n1)
        for copy in kv_in:
            copy.wait_recv()
        ld_ct.wait()
        total = R.kvb[k.c, k.z].astype(F32) + R.kvct_v[...]
        for d in range(3):
            total = total + R.kvi[d].astype(F32)
        own = rows(k.t, 128)
        cos, sin = cos_sin(R.csv, own)
        R.dkvs[:, 0:128] = turn(total[:, 0:128], cos, -sin).astype(BF16)
        R.dkvs[:, 128:256] = total[:, 128:256].astype(BF16)
        dkw = R.q
        dkw[own] = R.dkvs[...]
        dk_in = [k.go(R.dkvs, dkw.at[own], k.zdev(d)) for d in (1, 2, 3)]
        dk_sib = [k.go(R.dkvs, dkw.at[own], k.sib())]
        gi = GatherZ(k, R.ig, R.xs)

        def shard3(i):
            s = rows(i, 32)
            d = R.h1[s] + dot(R.dkvs[s], R.wqkv[:, 256:512], NT)
            y1, r1 = unit(R.xs[s].astype(F32))
            R.xs[s] = (R.dh1[s] + norm_back(d, R.gain1[...], y1, r1)).astype(BF16)
            dy = d * y1
            R.gn[1] += dy[0:8] + dy[8:16] + dy[16:24] + dy[24:32]

        loop(4, shard3)
        gi.start()
        st_ig = local(R.xs, R.ig.at[k.t])
        sm = gm.at[1]
        two = [jnp.sum(R.gn[i], axis=0, keepdims=True) for i in (1, 0)]
        two = jnp.concatenate(two + [jnp.zeros((14, 2048), F32)], axis=0).astype(BF16)
        for e in range(16):
            sm[e // 4, e % 4, 256:272] = two[:, 128 * e:128 * e + 128]
        line = pl.ds(256, 16)
        nx = [k.go(sm.at[(k.x + d) % 4, :, line], R.nvx.at[d - 1], k.xdev(d)) for d in (1, 2, 3)]
        for copy in dk_in:
            copy.wait_recv()
        theirs = [dkw.at[rows(k.slot(d), 128)] for d in (1, 2, 3)]
        dk_sib += [k.go(piece, piece, k.sib()) for piece in theirs]
        next(xy_att, None)
        next(xy_up, None)
        go.share_far()
        for copy in nx:
            copy.wait_recv()
        R.nvs[...] = (sm[k.x, :, line].astype(F32) + sum(R.nvx[i].astype(F32) for i in range(3))).astype(BF16)
        ny = [k.go(R.nvs.at[(k.y + d) % 4], R.nvy.at[d - 1], k.ydev(d)) for d in (1, 2, 3)]
        for copy in dk_sib:
            copy.wait_recv()

        def grad_kv(n):
            res = dot(OC[:, :, rows(n, 256)].reshape(1024, 256), dkw[...], TN).astype(BF16)
            for e in range(16):
                dp = 2 * n + e // 8
                for half in range(2):
                    at = 32 * (e % 8) + 16 * half
                    sm[dp // 4, dp % 4, at:at + 16] = res[16 * e:16 * e + 16, 128 * half:128 * half + 128]

        loop(8, grad_kv)
        mine = pl.ds(pl.multiple_of(32 * k.t, 32), 32)
        x_in = [k.go(sm.at[(k.x + d) % 4, :, mine], R.kvx.at[d - 1], k.xdev(d)) for d in (1, 2, 3)]
        for copy in ny:
            copy.wait_recv()
        R.nvt[...] = (R.nvs[k.y].astype(F32) + sum(R.nvy[i].astype(F32) for i in range(3))).astype(BF16)
        peers = [k.slot(d) for d in (1, 2, 3)] + [k.slot(d, 1 - k.c) for d in (0, 1, 2, 3)]
        nt = [k.go(R.nvt, R.nvr.at[i], (k.dp, peer)) for i, peer in enumerate(peers)]
        gi.forward()
        for copy in x_in:
            copy.wait_recv()
        R.kvx[3] = (sm[k.x, :, mine].astype(F32) + sum(R.kvx[i].astype(F32) for i in range(3))).astype(BF16)
        y_in = [k.go(R.kvx.at[3, (k.y + d) % 4], R.kvy.at[d - 1], k.ydev(d)) for d in (1, 2, 3)]
        next(xy_att, None)
        next(xy_up, None)
        gi.share_near()
        for copy in y_in + nt:
            copy.wait_recv()
        whole = R.kvx[3, k.y].astype(F32) + sum(R.kvy[i].astype(F32) for i in range(3))
        for n in range(2):
            R.kvsum[:, 128 * n:128 * n + 128] = whole[16 * n:16 * n + 16]
        gains = R.nvt[...].astype(F32) + sum(R.nvr[i].astype(F32) for i in range(7))
        R.kvsum[:, 256:384] = pltpu.roll(gains, (128 - 16 * k.t) % 128, axis=1)
        next(xy_att, None)
        for xy in (xy_att, xy_up):
            for _ in xy:
                pass
        gi.share_far()
        for ag in (go, gi):
            for d in (0, 1, 3, 2):
                ag.ready(d)
        for copy in w_x + w_y + [w_core] + sent_c + sent_d + dq_in + kv_in + dk_in + dk_sib + nx + ny + nt + x_in + y_in + [kv_swap]:
            copy.wait_send()
        for item in (gd, ou, gi, go):
            item.drain()
        for copy in (st_ig, st_out, kept[0], kept[1]):
            copy.wait()

    R.stage2[...] = OC[k.t]
    pl.run_scoped(weights, pltpu.VMEM((3, 4, 4, 704, 128), BF16))
    st_kv.wait()


def b16(*s):
    return pltpu.VMEM(s, BF16)


def b32(*s):
    return pltpu.VMEM(s, F32)


def angle_table():
    inverse = np.exp(np.arange(64) * (-2.0 * math.log(10000.0) / 128))
    angle = np.arange(1024)[:, None] * inverse
    return np.concatenate([np.cos(angle), np.sin(angle)], axis=1).astype(np.float32)


def per_device(
    inputs, doc_lengths, norm1_gain, w_query, w_shared_kv, w_output, norm2_gain,
    w_gate, w_up, w_down, out_cotangent, kv_cotangent,
):
    cut = lambda v: v.reshape(8, 128, v.shape[-1])
    ins = [
        cut(inputs), cut(out_cotangent), w_query, w_shared_kv, w_output, w_gate.T, w_up.T, w_down,
        cut(kv_cotangent), jnp.asarray(angle_table()), norm1_gain.reshape(1, 2048), norm2_gain.reshape(1, 2048),
        doc_lengths,
    ]
    wide = ((8, 128, 2048), BF16)
    outs = [
        wide, wide, ((1024, 256), BF16), ((2624, 128), F32), ((16, 384), F32), wide, ((8, 128, 1536), BF16),
        ((4, 2, 2, 128, 2048), BF16),
    ]
    big = b16(8, 128, 2048)
    hops = [b16(64, 2048), b16(64, 2048), b16(128, 2048), b16(128, 2048)]
    core = b16(4, 128, 2048)
    scratch = (
        [big] * 5 + [core] + hops + hops
        + [b32(128, 2048), b32(128, 2048), b16(128, 2048), b16(128, 2048)]
        + [b16(2048, 512), b16(256, 2048), b16(1024, 256), b16(1024, 256), b16(1024, 256), b16(1024, 256)]
        + [b32(1024, 256), b32(1024, 256), b16(1024, 704), b16(1024, 704), b16(1024, 704), b32(2, 8, 2048)]
        + [b16(2, 4, 128, 256), b16(4, 128, 256), b16(3, 128, 256), b16(128, 256)]
        + [b16(8, 128, 256), b16(4, 4, 32, 128), b16(3, 32, 128)]
        + [b16(3, 4, 16, 128), b16(4, 16, 128), b16(3, 16, 128), b16(16, 128), b16(7, 16, 128)]
        + [b32(128, 256), b32(2, 352, 128), pltpu.SemaphoreType.REGULAR] + [pltpu.SemaphoreType.REGULAR] + [pltpu.SemaphoreType.DMA((40,))]
        + [pltpu.SemaphoreType.DMA((NSEM,)), pltpu.SemaphoreType.DMA((NSEM,))]
        + grads_bufs(704) + grads_bufs(704)
    )
    output, input_grad, shared_kv, gsum, kvsum, *_ = pl.pallas_call(
        block,
        out_shape=[jax.ShapeDtypeStruct(s, d) for s, d in outs],
        in_specs=[ANY] * 10 + [VM] * 2 + [pl.BlockSpec(memory_space=pltpu.SMEM)],
        out_specs=[ANY] * 4 + [VM] + [ANY] * 3,
        scratch_shapes=scratch,
        compiler_params=pltpu.CompilerParams(
            collective_id=0, has_side_effects=True, vmem_limit_bytes=VLIM
        ),
    )(*ins)
    shapes = [
        ((1024, 2048), BF16), ((1024, 2048), BF16), ((1024, 256), BF16), ((128, 256), F32), ((256, 128), F32),
        ((704, 128), F32), ((704, 128), F32), ((704, 128), F32),
    ]
    flat = lambda v: v.reshape(1024, 2048)
    output, input_grad, shared_kv, g_query, g_out, g_gate, g_up, g_down = pl.pallas_call(
        finish,
        out_shape=[jax.ShapeDtypeStruct(s, d) for s, d in shapes],
        in_specs=[ANY] * 4,
        out_specs=[ANY] * 3 + [VM] + [ANY] * 4,
        scratch_shapes=[b16(8, 256, 2048), b16(1024, 256), b32(2624, 128), pltpu.SemaphoreType.DMA((2, 14))],
        compiler_params=pltpu.CompilerParams(vmem_limit_bytes=VLIM),
    )(flat(output), flat(input_grad), shared_kv, gsum)
    return (
        output, input_grad, shared_kv, kvsum[0, 256:272], g_query, kvsum[:, 0:256], g_out, kvsum[1, 256:272],
        g_gate.T, g_up.T, g_down,
    )


VLIM = 63 * 2**20 + 2**19


def solution(mesh):
    placed = (
        P("dp", None), P("dp", None), P(), P(None, "tensor"), P(), P("tensor", None), P(),
        P(None, "tensor"), P(None, "tensor"), P("tensor", None), P("dp", None), P("dp", None),
    )
    return jax.shard_map(
        per_device,
        mesh=mesh,
        in_specs=placed,
        out_specs=(
            P("dp", None), P("dp", None), P("dp", None), P(("dp", "tensor")), P("dp", "tensor"),
            P(("dp", "tensor"), None), P("tensor", "dp"), P(("dp", "tensor")), P("dp", "tensor"),
            P("dp", "tensor"), P("tensor", "dp"),
        ),
        check_vma=False,
    )
```
